256 devices in a mesh: seq: 64 (over x, z, core), head: 4 (over y).
Axes of the slice: x: 4, y: 4, z: 8, core: 2. Of those that a mesh axis runs over, the one named last changes fastest.
Arguments:
- feat_q: bfloat16 [65536, 256], P('seq', 'head'), may hold values from -6 to 6
- feat_k: bfloat16 [65536, 256], P('seq', 'head'), may hold values from -6 to 6
- values: bfloat16 [65536, 2048], P('seq', 'head'), may hold values from -6 to 6
- win_q: bfloat16 [65536, 2048], P('seq', 'head'), may hold values from -6 to 6
- win_k: bfloat16 [65536, 2048], P('seq', 'head'), may hold values from -6 to 6
- win_v: bfloat16 [65536, 2048], P('seq', 'head'), may hold values from -6 to 6
- head_gain: float32 [16], P('head'), may hold values from 0.8 to 3.8
Outputs:
- mixed: bfloat16 [65536, 2048], P('seq', 'head')
The draws below stay inside these ranges and needn't reach their ends.
All inputs are finite; a program needn't handle non-finite values.
Results may differ from the reference program's by a relative error of at most 0.0032.
Values may be sent and summed in bfloat16 or wider, within the bound.
A program may use at most 128 MiB of HBM per device.

```python
import math
import jax
import jax.numpy as jnp
from jax import lax

H = 16
HD = 128
FEAT = 16
W = 64
BLOCK = 512
TOK_DEV = 1024
TOKENS = 65536


def draw_win_q(key, part):
    key = jax.random.fold_in(key, 21)
    base = jnp.clip(jax.random.normal(key, (TOKENS, H * HD), jnp.float32), -6.0, 6.0)
    return base.astype(jnp.bfloat16)


def draw_win_k(key, part):
    key = jax.random.fold_in(key, 22)
    base = jnp.clip(jax.random.normal(key, (TOKENS, H * HD), jnp.float32), -6.0, 6.0)
    return base.astype(jnp.bfloat16)


def draw_head_gain(key, part):
    key = jax.random.fold_in(key, 23)
    ramp = 2.0 ** (1.6 * jnp.arange(H, dtype=jnp.float32) / (H - 1))
    return ramp * jax.random.uniform(key, (H,), jnp.float32, 0.8, 1.25)


def draw_feat_k(key, part):
    key = jax.random.fold_in(key, 24)
    keys = jax.random.split(key, 5)
    shard_count = TOKENS // TOK_DEV
    levels = jnp.exp(jax.random.uniform(keys[0], (shard_count, H), jnp.float32, -0.8, 0.8))
    row_levels = jnp.repeat(levels, TOK_DEV, axis=0)
    mean_signs = jnp.where(jax.random.bernoulli(keys[1], 0.5, (H, FEAT)), 1.0, -1.0).astype(jnp.float32)
    loadings = jnp.where(jax.random.bernoulli(keys[2], 0.5, (H, FEAT)), 0.5, -0.5).astype(jnp.float32)
    noise = 0.85 * jnp.clip(jax.random.normal(keys[3], (TOKENS, H, FEAT), jnp.float32), -4.0, 4.0)
    common = jnp.clip(jax.random.normal(keys[4], (TOKENS, H, 1), jnp.float32), -4.0, 4.0)
    offset = 0.7
    mixed_rows = row_levels[:, :, None] * (noise + common * loadings[None] + offset * mean_signs[None])
    return jnp.clip(mixed_rows, -6.0, 6.0).reshape(TOKENS, H * FEAT).astype(jnp.bfloat16)


def draw_values(key, part):
    key = jax.random.fold_in(key, 25)
    keys = jax.random.split(key, 3)
    shard_count = TOKENS // TOK_DEV
    channel_signs = jnp.where(jax.random.bernoulli(keys[0], 0.5, (H * HD,)), 1.0, -1.0).astype(jnp.float32)
    shard_means = 0.6 * jnp.clip(jax.random.normal(keys[1], (shard_count, H * HD), jnp.float32), -3.0, 3.0)
    fraction = jnp.arange(TOKENS, dtype=jnp.float32) / TOKENS
    trend = 2.0 * jnp.exp(-4.0 * fraction)[:, None] * channel_signs[None, :]
    noise = jnp.clip(jax.random.normal(keys[2], (TOKENS, H * HD), jnp.float32), -3.5, 3.5)
    rows = noise + trend + jnp.repeat(shard_means, TOK_DEV, axis=0)
    return jnp.clip(rows, -6.0, 6.0).astype(jnp.bfloat16)


def block_scale(rng, dims, shards, smallest, top_value):
    loudness = 1.0
    for position, shards_of in shards:
        steps = jax.random.uniform(jax.random.fold_in(jax.random.fold_in(rng, 6), position), (shards_of,), jnp.float32, smallest / len(shards), top_value / len(shards))
        loudness = loudness * jnp.repeat(jnp.exp(steps), dims[position] // shards_of).reshape((-1,) + (1,) * (len(dims) - 1 - position))
    return loudness


def scatter_about(key, shape, width, limit, shards=(), kind=jnp.bfloat16):
    loudness = block_scale(key, shape, shards, -0.22, 0.18) if shards else 1.0
    entries = jax.random.normal(key, shape, jnp.float32) * width * loudness
    return jnp.minimum(jnp.maximum(entries, -limit), limit).astype(kind)


def setup_inputs(seed: int = 0) -> dict:
    streams_of = jax.random.split(jax.random.key(seed), 8)
    feat_q = scatter_about(streams_of[0], (TOKENS, H * FEAT), 1.0, 6.0, ((0, 64), (1, 4)))
    feat_k = draw_feat_k(jax.random.fold_in(streams_of[7], 71), 0)
    values = draw_values(jax.random.fold_in(streams_of[7], 71), 0)
    win_q = draw_win_q(jax.random.fold_in(streams_of[7], 71), 0)
    win_k = draw_win_k(jax.random.fold_in(streams_of[7], 71), 0)
    win_v = scatter_about(streams_of[5], (TOKENS, H * HD), 1.0, 6.0, ((0, 64), (1, 4)))
    head_gain = draw_head_gain(jax.random.fold_in(streams_of[7], 71), 0)
    return {"feat_q": feat_q, "feat_k": feat_k, "values": values, "win_q": win_q, "win_k": win_k, "win_v": win_v, "head_gain": head_gain}


quad_scale = 1.0 / (4.0 * math.sqrt(2.0))
eps = 1e-06
highest_setting = lax.Precision.HIGHEST

def feature_map(inputs):
    widened = inputs.astype(jnp.float32)
    feat_size = widened.shape[-1]
    quadratic = (widened[..., :, None] * widened[..., None, :]).reshape(widened.shape[:-1] + (feat_size * feat_size,)) * quad_scale
    constant = jnp.ones(widened.shape[:-1] + (1,), jnp.float32)
    return jnp.concatenate([constant, widened * 0.5, quadratic], axis=-1).astype(jnp.bfloat16)

def reference(feat_q, feat_k, values, win_q, win_k, win_v, head_gain):
    tok_total = values.shape[0]
    head_count = head_gain.shape[0]
    head_size = values.shape[1] // head_count
    feat_size = feat_q.shape[1] // head_count
    feat_len = 1 + feat_size + feat_size * feat_size
    block_count = tok_total // BLOCK
    padded_k = jnp.concatenate([jnp.zeros((W, win_k.shape[1]), win_k.dtype), win_k], axis=0)
    padded_v = jnp.concatenate([jnp.zeros((W, win_v.shape[1]), win_v.dtype), win_v], axis=0)
    row_ids = jnp.arange(BLOCK, dtype=jnp.int32)[:, None]
    col_ids = jnp.arange(BLOCK + W, dtype=jnp.int32)[None, :]
    causal = row_ids >= jnp.arange(BLOCK, dtype=jnp.int32)[None, :]
    band = (col_ids <= row_ids + W) & (col_ids > row_ids)
    gains = head_gain.astype(jnp.float32)[None, :, None]

    def advance(carry, block):
        running_state, normal = carry
        start = (block * BLOCK).astype(jnp.int32)
        query_features = lax.dynamic_slice_in_dim(feat_q, start, BLOCK, 0).reshape(BLOCK, head_count, feat_size)
        key_features = lax.dynamic_slice_in_dim(feat_k, start, BLOCK, 0).reshape(BLOCK, head_count, feat_size)
        value_rows = lax.dynamic_slice_in_dim(values, start, BLOCK, 0).reshape(BLOCK, head_count, head_size).astype(jnp.float32)
        map_q = lax.optimization_barrier(feature_map(query_features)).astype(jnp.float32)
        mapped_keys = lax.optimization_barrier(feature_map(key_features)).astype(jnp.float32)
        common_range = jnp.einsum('cau,bau->acb', query_features.astype(jnp.float32), key_features.astype(jnp.float32), precision=highest_setting)
        kernel = jnp.where(causal[None], 1.0 + common_range * 0.25 + common_range * common_range / 32.0, 0.0).astype(jnp.bfloat16)
        kernel = lax.optimization_barrier(kernel).astype(jnp.float32)
        numer = jnp.einsum('hqk,khd->qhd', kernel, value_rows, precision=highest_setting) + jnp.einsum('qhf,hfd->qhd', map_q, running_state, precision=highest_setting)
        denom = lax.optimization_barrier(jnp.sum(kernel, axis=2)).T + jnp.einsum('qhf,hf->qh', map_q, normal, precision=highest_setting)
        linear = numer / denom[..., None]
        running_state = running_state + jnp.einsum('rlb,rlg->lbg', mapped_keys, value_rows, precision=highest_setting)
        normal = normal + lax.optimization_barrier(jnp.sum(mapped_keys, axis=0))
        queries = lax.dynamic_slice_in_dim(win_q, start, BLOCK, 0).reshape(BLOCK, head_count, head_size).astype(jnp.float32)
        keys = lax.dynamic_slice_in_dim(padded_k, start, BLOCK + W, 0).reshape(BLOCK + W, head_count, head_size).astype(jnp.float32)
        wvals = lax.dynamic_slice_in_dim(padded_v, start, BLOCK + W, 0).reshape(BLOCK + W, head_count, head_size).astype(jnp.float32)
        scores = jnp.einsum('qhd,khd->hqk', queries, keys, precision=highest_setting) / math.sqrt(head_size)
        valid = band & (start - W + col_ids >= 0)
        scores = jnp.where(valid[None], scores, -1e+30)
        peak = lax.optimization_barrier(jnp.max(scores, axis=2, keepdims=True))
        weights = jnp.exp(scores - peak)
        weights = weights / lax.optimization_barrier(jnp.sum(weights, axis=2, keepdims=True))
        weights = lax.optimization_barrier(weights.astype(jnp.bfloat16)).astype(jnp.float32)
        window = jnp.einsum('hqk,khd->qhd', weights, wvals, precision=highest_setting)
        combined = (gains * (linear + window)).reshape(BLOCK, head_count * head_size)
        power = lax.optimization_barrier(jnp.mean(combined * combined, axis=1, keepdims=True))
        mixed = (combined * lax.rsqrt(power + eps)).astype(jnp.bfloat16)
        return ((running_state, normal), mixed)
    start_carry = (jnp.zeros((head_count, feat_len, head_size), jnp.float32), jnp.zeros((head_count, feat_len), jnp.float32))
    final_carry, outputs = lax.scan(advance, start_carry, jnp.arange(block_count, dtype=jnp.int32))
    return outputs.reshape(tok_total, head_count * head_size)
```

```python
import functools
import math

import jax
import jax.numpy as jnp
import numpy as np
from jax import lax
from jax.experimental import pallas as pl
from jax.experimental.pallas import tpu as pltpu
from jax.sharding import PartitionSpec as P

MESH = pl.DeviceIdType.MESH
F32 = jnp.float32
BF16 = jnp.bfloat16

W = 64
BLOCK = 512
FEAT = 16
HD = 128
ROWS = 160
PIECE = 16
QUAD = 1.0 / (4.0 * math.sqrt(2.0))
EPS = 1e-06


def feature_tables(heads):
    ones_lane = heads * FEAT
    first = np.zeros((heads, ROWS, 128), np.float32)
    second = np.zeros((heads, ROWS, 128), np.float32)
    scale_k = np.zeros((ROWS,), np.float32)
    scale_q = np.zeros((ROWS,), np.float32)
    row = 0
    for shift in range(FEAT // 2 + 1):
        for a in range(FEAT if shift < FEAT // 2 else FEAT // 2):
            for h in range(heads):
                first[h, row, h * FEAT + a] = 1.0
                second[h, row, h * FEAT + (a + shift) % FEAT] = 1.0
            scale_k[row] = QUAD
            scale_q[row] = np.float32(QUAD) * (1.0 if shift == 0 else 2.0)
            row += 1
    for a in range(FEAT):
        for h in range(heads):
            first[h, row, h * FEAT + a] = 1.0
            second[h, row, ones_lane] = 1.0
        scale_k[row] = scale_q[row] = 0.5
        row += 1
    first[:, row, ones_lane] = 1.0
    second[:, row, ones_lane] = 1.0
    scale_k[row] = scale_q[row] = 1.0
    row += 1
    assert row + 2 <= ROWS
    wide_k = np.broadcast_to(scale_k[:, None], (ROWS, 128))
    wide_q = np.broadcast_to(scale_q[None, :], (8, ROWS))
    return first, second, np.ascontiguousarray(wide_k), np.ascontiguousarray(wide_q), row


def dot(a, b):
    return jnp.dot(a, b, preferred_element_type=F32)


def dot_nt(a, b):
    return lax.dot_general(a, b, (((1,), (1,)), ((), ())), preferred_element_type=F32)


def split(x):
    high = x.astype(BF16)
    return high, (x - high.astype(F32)).astype(BF16)


def mixer(
    dims,
    fq_hbm, fk_hbm, v_hbm, wq_hbm, wk_hbm, wv_hbm, gain, ea_hbm, eb_hbm, sk_hbm, sq_hbm,
    out_hbm,
    fq, fk, v, wq, wk, wv, ea, eb, sk, sq,
    edge_k, edge_v, first_state, total, got, chip_sum, gathered, prefixes, arrived, payload, before,
    local, window, map_q, power_own, power_all, squares, out,
    in_sem, out_sem, send_sem, recv_sem,
):
    seq_n, head_n, z_n, heads, tokens, normal_row = dims
    chips = seq_n // 2
    half = heads // 2
    pieces = half * ROWS // PIECE
    blocks = tokens // BLOCK
    me, head = lax.axis_index("seq"), lax.axis_index("head")
    core = lax.rem(me, 2)
    chip = me // 2
    other = me + 1 - 2 * core

    def load(index, src, dst):
        return pltpu.make_async_copy(src, dst, in_sem.at[index])

    loads = [
        load(0, fk_hbm, fk),
        load(1, ea_hbm, ea), load(2, eb_hbm, eb), load(3, sk_hbm, sk),
        load(4, v_hbm, v), load(5, fq_hbm, fq), load(6, sq_hbm, sq),
        load(7, wk_hbm, wk), load(8, wq_hbm, wq), load(9, wv_hbm, wv),
    ]
    for copy in loads:
        copy.start()

    def remote(src, dst, index, seq, group):
        return pltpu.make_async_remote_copy(
            src_ref=src, dst_ref=dst, send_sem=send_sem.at[index], recv_sem=recv_sem.at[index],
            device_id=(seq, group), device_id_type=MESH,
        )

    def settle(buffer, count, sem):
        pltpu.make_async_copy(buffer.at[pl.ds(0, count)], buffer.at[pl.ds(0, count)], sem).wait()

    barrier = pltpu.get_barrier_semaphore()
    edge_mate = lax.rem(me + 2 * core - 1 + seq_n, seq_n)

    def greet(seq, group):
        pl.semaphore_signal(barrier, inc=1, device_id=(seq, group), device_id_type=MESH)

    greet(other, head)
    greet(edge_mate, head)
    for step in range(1, head_n):
        greet(me, lax.rem(head + step, head_n))

    def greet_chip(step, carry):
        greet(2 * lax.rem(chip + step, chips) + core, head)
        return carry

    lax.fori_loop(1, chips, greet_chip, 0)

    lanes = lax.broadcasted_iota(jnp.int32, (128, 128), 1)
    subs = lax.broadcasted_iota(jnp.int32, (128, 128), 0)
    eye = lanes == subs
    ones_v = jnp.ones((BLOCK, HD), BF16)
    tail = jnp.where(lax.broadcasted_iota(jnp.int32, (BLOCK, 128 - heads * FEAT), 1) == 0, 1.0, 0.0).astype(BF16)
    for index in range(4):
        loads[index].wait()
    loads[4].wait()

    def with_one(ref, start):
        return jnp.concatenate([ref[pl.ds(start, BLOCK), :], tail], axis=1)

    def state_of(h):
        cols = pl.ds(pl.multiple_of(h * HD, HD), HD)
        summed = None
        for block in range(blocks):
            keys = with_one(fk, block * BLOCK)
            scale = sk[...]
            mapped = dot_nt(ea[h], keys) * dot_nt(eb[h], keys)
            mapped = (mapped * jnp.concatenate([scale] * (BLOCK // 128), axis=1)).astype(BF16)
            both = dot(mapped, jnp.concatenate([v[pl.ds(block * BLOCK, BLOCK), cols], ones_v], axis=1))
            state, normal = both[:, :HD], both[:, HD:]
            low = jnp.sum(jnp.where(eye, normal[:128], 0.0), axis=0, keepdims=True)
            high = jnp.sum(jnp.where(eye[: ROWS - 128], normal[128:], 0.0), axis=0, keepdims=True)
            row_ids = lax.broadcasted_iota(jnp.int32, (ROWS, HD), 0)
            state = jnp.where(row_ids == normal_row, low, jnp.where(row_ids == normal_row + 1, high, state))
            if block == 0:
                first_state[h] = state
            summed = state if summed is None else summed + state
        per_head = ROWS // PIECE
        total[pl.ds(h * per_head, per_head)] = summed.reshape(per_head, PIECE, HD)

    def states(start):
        def body(i, carry):
            state_of(start + i)
            return carry
        lax.fori_loop(0, half, body, 0)

    states(half * (1 - core))
    pl.semaphore_wait(barrier, 1 + 1 + head_n - 1 + chips - 1)
    swap_out = remote(total.at[pl.ds((1 - core) * pieces, pieces)], got, 0, other, head)
    swap_out.start()
    states(half * core)

    following = lax.rem(me + 1, seq_n)
    edges = [
        remote(wk_hbm.at[pl.ds(tokens - W, W)], edge_k, 1, following, head),
        remote(wv_hbm.at[pl.ds(tokens - W, W)], edge_v, 2, following, head),
    ]
    for copy in edges:
        copy.start()
    swap_out.wait_recv()
    own = pl.ds(core * pieces, pieces)
    chip_sum[...] = total[own] + got[...]

    def owner_chip(k):
        return lax.rem(k, chips // z_n) * z_n + k // (chips // z_n)

    owned = lax.rem(chip, z_n) * (chips // z_n) + chip // z_n
    is_owner = owned < pieces

    def send_piece(i, carry):
        k = lax.rem(owned + i, pieces)

        @pl.when(owner_chip(k) != chip)
        def _():
            remote(chip_sum.at[k], gathered.at[chip], 3, 2 * owner_chip(k) + core, head).start()
        return carry

    lax.fori_loop(0, pieces, send_piece, 0)

    for index in (5, 6, 7, 8, 9):
        loads[index].wait()
    quarter = BLOCK // 2
    tri = lax.broadcasted_iota(jnp.int32, (quarter, quarter), 0) >= lax.broadcasted_iota(jnp.int32, (quarter, quarter), 1)
    feat_lane = lax.broadcasted_iota(jnp.int32, (1, heads * FEAT), 1)

    def within(i, carry):
        h, block = i // blocks, lax.rem(i, blocks)
        cols = pl.ds(pl.multiple_of(h * HD, HD), HD)
        start = pl.multiple_of(block * BLOCK, BLOCK)
        keys = fk[pl.ds(start, BLOCK), :]
        mine = jnp.where(feat_lane // FEAT == h, 1.0, 0.0).astype(BF16)
        queries = fq[pl.ds(start, BLOCK), :] * mine
        vals = jnp.concatenate([v[pl.ds(start, BLOCK), cols], ones_v], axis=1)

        def weights(q, k):
            s = dot_nt(q, k)
            return 1.0 + s * 0.25 + s * s * (1.0 / 32.0)

        top = jnp.where(tri, weights(queries[:quarter], keys[:quarter]), 0.0).astype(BF16)
        local[h, pl.ds(start, quarter), :] = dot(top, vals[:quarter])
        left = weights(queries[quarter:], keys[:quarter]).astype(BF16)
        right = jnp.where(tri, weights(queries[quarter:], keys[quarter:]), 0.0).astype(BF16)
        local[h, pl.ds(start + quarter, quarter), :] = dot(jnp.concatenate([left, right], axis=1), vals)
        ext = with_one(fq, start)
        mapped = dot_nt(ext, ea[h]) * dot_nt(ext, eb[h]) * sq[0:1, :]
        map_q[h, pl.ds(start, BLOCK), :] = mapped.astype(BF16)
        return carry

    lax.fori_loop(0, heads * blocks, within, 0)

    band_row = lax.broadcasted_iota(jnp.int32, (W, 2 * W), 0)
    band_col = lax.broadcasted_iota(jnp.int32, (W, 2 * W), 1)
    band = (band_col > band_row) & (band_col <= band_row + W)
    sharp = 1.0 / math.sqrt(HD)

    def attend(scores, allowed):
        scores = jnp.where(allowed, scores * sharp, -1e30)
        weights = jnp.exp(scores - jnp.max(scores, axis=1, keepdims=True))
        return (weights / jnp.sum(weights, axis=1, keepdims=True)).astype(BF16)

    group = 4
    band_group = jnp.concatenate([band] * group, axis=0)

    def windows(h, first, count):
        cols = pl.ds(pl.multiple_of(h * HD, HD), HD)
        starts = [first + c * W for c in range(count)]
        scores = [
            dot_nt(wq[pl.ds(s, W), cols], wk[pl.ds(s - W, 2 * W), cols]) for s in starts
        ]
        probs = attend(jnp.concatenate(scores, axis=0), band_group[: count * W])
        for c, s in enumerate(starts):
            window[pl.ds(s, W), cols] = dot(probs[c * W : (c + 1) * W], wv[pl.ds(s - W, 2 * W), cols])

    def window_head(h, carry):
        windows(h, W, group - 1)

        def rest(g, inner):
            windows(h, pl.multiple_of(g * group * W, group * W), group)
            return inner

        return lax.fori_loop(1, tokens // (group * W), rest, carry)

    lax.fori_loop(0, heads, window_head, 0)

    edges[0].wait_recv()
    edges[1].wait_recv()
    band_first = band & ((band_col >= W) | (me > 0))

    def window_edge(h, carry):
        cols = pl.ds(pl.multiple_of(h * HD, HD), HD)
        keys = jnp.concatenate([edge_k[:, cols], wk[pl.ds(0, W), cols]], axis=0)
        vals = jnp.concatenate([edge_v[:, cols], wv[pl.ds(0, W), cols]], axis=0)
        probs = attend(dot_nt(wq[pl.ds(0, W), cols], keys), band_first)
        window[pl.ds(0, W), cols] = dot(probs, vals)
        return carry

    lax.fori_loop(0, heads, window_edge, 0)

    @pl.when(is_owner)
    def _():
        gathered[chip] = chip_sum[owned]
        settle(gathered, chips - 1, recv_sem.at[3])

        def add(u, run):
            prefixes[u] = run
            return run + gathered[u]

        lax.fori_loop(0, chips, add, jnp.zeros((PIECE, HD), F32))

        def send_prefix(i, carry):
            u = lax.rem(chip + i, chips)
            remote(prefixes.at[u], arrived.at[owned], 4, 2 * u + core, head).start()
            return carry

        lax.fori_loop(1, chips, send_prefix, 0)
        arrived[owned] = prefixes[chip]
        settle(arrived, pieces - 1, recv_sem.at[4])

    @pl.when(jnp.logical_not(is_owner))
    def _():
        settle(arrived, pieces, recv_sem.at[4])

    ahead = jnp.where(core == 0, 1.0, 0.0)
    payload[...] = arrived[...] + total[own] * ahead
    swap_back = remote(payload, before.at[own], 5, other, head)
    swap_back.start()
    before[own] = arrived[...] + got[...] * (1.0 - ahead)

    per_head = ROWS // PIECE

    def finish(h, block, fresh):
        cols = pl.ds(pl.multiple_of(h * HD, HD), HD)
        rows = pl.ds(block * BLOCK, BLOCK)
        state = before[pl.ds(h * per_head, per_head)].reshape(ROWS, HD)
        if block > 0:
            state = state + first_state[h]
        normal = jnp.concatenate(
            [
                jnp.broadcast_to(state[normal_row : normal_row + 1], (HD, HD)).T,
                jnp.broadcast_to(state[normal_row + 1 : normal_row + 2], (HD, HD)).T[: ROWS - HD],
            ],
            axis=0,
        )
        high, low = split(jnp.concatenate([state, normal], axis=1))
        mapped = map_q[h, rows, :]
        sums = dot(mapped, high) + dot(mapped, low) + local[h, rows, :]
        combined = gain[h] * (sums[:, :HD] / sums[:, HD:] + window[rows, cols])
        window[rows, cols] = combined
        squared = combined * combined
        squares[rows, :] = squared if fresh else squares[rows, :] + squared

    own_head = half * core
    for block in range(blocks):
        finish(own_head, block, True)
    for i in range(1, half):
        for block in range(blocks):
            finish(own_head + i, block, False)
    swap_back.wait_recv()
    for block in range(blocks):
        for i in range(half):
            finish(half * (1 - core) + i, block, False)
        sums = jnp.sum(squares[pl.ds(block * BLOCK, BLOCK), :], axis=1, keepdims=True)
        for r in range(BLOCK // 128):
            wide = jnp.broadcast_to(sums[r * 128 : (r + 1) * 128], (128, 128))
            power_own[block, r : r + 1, :] = jnp.sum(jnp.where(eye, wide, 0.0), axis=0, keepdims=True)
        power_all[block, head] = power_own[block]
        for step in range(1, head_n):
            remote(
                power_own.at[block], power_all.at[block, head], 6 + block, me, lax.rem(head + step, head_n)
            ).start()

    stores = []
    for block in range(blocks):
        rows = pl.ds(block * BLOCK, BLOCK)
        settle(power_all.at[block], head_n - 1, recv_sem.at[6 + block])
        power = jnp.sum(power_all[block], axis=0) * (1.0 / (heads * head_n * HD))
        factor = lax.rsqrt(power + EPS)
        for r in range(BLOCK // 128):
            some = pl.ds(block * BLOCK + r * 128, 128)
            column = jnp.broadcast_to(factor[r : r + 1], (128, 128)).T
            out[some, :] = (window[some, :] * jnp.concatenate([column] * heads, axis=1)).astype(BF16)
        store = pltpu.make_async_copy(out.at[rows], out_hbm.at[rows], out_sem.at[block])
        store.start()
        stores.append(store)

    swap_out.wait_send()
    for copy in edges:
        copy.wait_send()
    swap_back.wait_send()

    @pl.when(is_owner)
    def _():
        settle(arrived, pieces - 1, send_sem.at[3])
        settle(gathered, chips - 1, send_sem.at[4])

    @pl.when(jnp.logical_not(is_owner))
    def _():
        settle(arrived, pieces, send_sem.at[3])

    for block in range(blocks):
        settle(power_all.at[block], head_n - 1, send_sem.at[6 + block])
    for store in stores:
        store.wait()


def solution(mesh):
    seq_n, head_n = mesh.shape["seq"], mesh.shape["head"]
    z_n = 8

    def local(feat_q, feat_k, values, win_q, win_k, win_v, head_gain):
        tokens, width = values.shape
        heads = head_gain.shape[0]
        first, second, scale_k, scale_q, normal_row = feature_tables(heads)
        chips = seq_n // 2
        pieces = heads // 2 * ROWS // PIECE
        blocks = tokens // BLOCK
        dims = (seq_n, head_n, z_n, heads, tokens, normal_row)
        anywhere = pl.BlockSpec(memory_space=pl.ANY)
        vm = pltpu.VMEM
        return pl.pallas_call(
            functools.partial(mixer, dims),
            out_shape=jax.ShapeDtypeStruct((tokens, width), BF16),
            in_specs=[anywhere] * 6 + [pl.BlockSpec(memory_space=pltpu.SMEM)] + [anywhere] * 4,
            out_specs=anywhere,
            scratch_shapes=[
                vm(feat_q.shape, BF16), vm(feat_k.shape, BF16),
                vm(values.shape, BF16), vm(values.shape, BF16), vm(values.shape, BF16), vm(values.shape, BF16),
                vm((heads, ROWS, 128), BF16), vm((heads, ROWS, 128), BF16), vm((ROWS, 128), F32), vm((8, ROWS), F32),
                vm((W, width), BF16), vm((W, width), BF16),
                vm((heads, ROWS, HD), F32),
                vm((2 * pieces, PIECE, HD), F32),
                vm((pieces, PIECE, HD), F32),
                vm((pieces, PIECE, HD), F32),
                vm((chips, PIECE, HD), F32),
                vm((chips, PIECE, HD), F32),
                vm((pieces, PIECE, HD), F32),
                vm((pieces, PIECE, HD), F32),
                vm((2 * pieces, PIECE, HD), F32),
                vm((heads, tokens, 2 * HD), F32),
                vm((tokens, width), F32),
                vm((heads, tokens, ROWS), BF16),
                vm((blocks, BLOCK // 128, 128), F32),
                vm((blocks, head_n, BLOCK // 128, 128), F32),
                vm((tokens, HD), F32),
                vm((tokens, width), BF16),
                pltpu.SemaphoreType.DMA((10,)),
                pltpu.SemaphoreType.DMA((blocks,)),
                pltpu.SemaphoreType.DMA((6 + blocks,)),
                pltpu.SemaphoreType.DMA((6 + blocks,)),
            ],
            compiler_params=pltpu.CompilerParams(
                collective_id=0, has_side_effects=True, vmem_limit_bytes=48 * 2**20
            ),
            name="mixer",
        )(
            feat_q, feat_k, values, win_q, win_k, win_v, head_gain,
            jnp.asarray(first, BF16), jnp.asarray(second, BF16), jnp.asarray(scale_k), jnp.asarray(scale_q),
        )

    placed = (P("seq", "head"),) * 6 + (P("head"),)
    return jax.shard_map(local, mesh=mesh, in_specs=placed, out_specs=P("seq", "head"), check_vma=False)
```

```python
import functools
import math

import jax
import jax.numpy as jnp
import numpy as np
from jax import lax
from jax.experimental import pallas as pl
from jax.experimental.pallas import tpu as pltpu
from jax.sharding import PartitionSpec as P

MESH = pl.DeviceIdType.MESH
F32 = jnp.float32
BF16 = jnp.bfloat16

W = 64
BLOCK = 512
FEAT = 16
HD = 128
ROWS = 160
PIECE = 10
SLOT = 16
PIECES = ROWS // PIECE
WIDE = PIECES * SLOT
QUAD = 1.0 / (4.0 * math.sqrt(2.0))
EPS = 1e-06


def feature_tables(heads):
    ones_lane = heads * FEAT
    first = np.zeros((heads, ROWS, 128), np.float32)
    second = np.zeros((heads, ROWS, 128), np.float32)
    scale_k = np.zeros((ROWS,), np.float32)
    scale_q = np.zeros((ROWS,), np.float32)
    row = 0
    for shift in range(FEAT // 2 + 1):
        for a in range(FEAT if shift < FEAT // 2 else FEAT // 2):
            for h in range(heads):
                first[h, row, h * FEAT + a] = 1.0
                second[h, row, h * FEAT + (a + shift) % FEAT] = 1.0
            scale_k[row] = QUAD
            scale_q[row] = np.float32(QUAD) * (1.0 if shift == 0 else 2.0)
            row += 1
    for a in range(FEAT):
        for h in range(heads):
            first[h, row, h * FEAT + a] = 1.0
            second[h, row, ones_lane] = 1.0
        scale_k[row] = scale_q[row] = 0.5
        row += 1
    first[:, row, ones_lane] = 1.0
    second[:, row, ones_lane] = 1.0
    scale_k[row] = scale_q[row] = 1.0
    row += 1
    assert row + 2 <= ROWS
    spot = np.arange(ROWS) // PIECE * SLOT + np.arange(ROWS) % PIECE
    first_q = np.zeros((heads, WIDE, 128), np.float32)
    second_q = np.zeros((heads, WIDE, 128), np.float32)
    first_q[:, spot], second_q[:, spot] = first, second
    wide_k = np.ascontiguousarray(np.broadcast_to(scale_k[:, None], (ROWS, 128)))
    wide_q = np.zeros((8, WIDE), np.float32)
    wide_q[:, spot] = scale_q
    return first, second, first_q, second_q, wide_k, wide_q, row


def dot(a, b):
    return jnp.dot(a, b, preferred_element_type=F32)


def dot_nt(a, b):
    return lax.dot_general(a, b, (((1,), (1,)), ((), ())), preferred_element_type=F32)


def split(x):
    high = x.astype(BF16)
    return high, (x - high.astype(F32)).astype(BF16)


def mixer(
    dims,
    fq_hbm, fk_hbm, v_hbm, wq_hbm, wk_hbm, wv_hbm, gain, ea_hbm, eb_hbm, eaq_hbm, ebq_hbm, sk_hbm, sq_hbm,
    out,
    fq, fk, v, wq, wk, wv, ea, eb, eaq, ebq, sk, sq,
    edge_k, edge_v, first_state, total, got, chip_sum, gathered, prefixes, arrived, payload, before,
    fq_rows, local, window, map_q, power_own, power_all, squares,
    in_sem, send_sem, recv_sem,
):
    seq_n, head_n, z_n, heads, tokens, normal_row = dims
    x_n = seq_n // 2 // z_n
    chips = seq_n // 2
    half = heads // 2
    pieces = half * PIECES
    blocks = tokens // BLOCK
    me, head = lax.axis_index("seq"), lax.axis_index("head")
    core = lax.rem(me, 2)
    chip = me // 2
    other = me + 1 - 2 * core

    def load(index, src, dst):
        return pltpu.make_async_copy(src, dst, in_sem.at[index])

    loads = [
        load(0, fk_hbm, fk.at[pl.ds(0, heads * FEAT)]),
        load(1, ea_hbm, ea), load(2, eb_hbm, eb), load(3, sk_hbm, sk),
        load(4, v_hbm, v), load(5, fq_hbm, fq.at[pl.ds(0, heads * FEAT)]), load(6, sq_hbm, sq),
        load(10, eaq_hbm, eaq), load(11, ebq_hbm, ebq), load(7, wk_hbm, wk), load(8, wq_hbm, wq), load(9, wv_hbm, wv),
    ]
    for copy in loads:
        copy.start()

    def remote(src, dst, index, seq, group):
        return pltpu.make_async_remote_copy(
            src_ref=src, dst_ref=dst, send_sem=send_sem.at[index], recv_sem=recv_sem.at[index],
            device_id=(seq, group), device_id_type=MESH,
        )

    def settle(buffer, count, sem, rows=PIECE):
        part = buffer.at[pl.ds(0, count), pl.ds(0, rows)]
        pltpu.make_async_copy(part, part, sem).wait()

    barrier = pltpu.get_barrier_semaphore()
    edge_mate = lax.rem(me + 2 * core - 1 + seq_n, seq_n)

    def greet(seq, group):
        pl.semaphore_signal(barrier, inc=1, device_id=(seq, group), device_id_type=MESH)

    greet(other, head)
    greet(edge_mate, head)
    for step in range(1, head_n):
        greet(me, lax.rem(head + step, head_n))

    def greet_chip(step, carry):
        greet(2 * lax.rem(chip + step, chips) + core, head)
        return carry

    lax.fori_loop(1, chips, greet_chip, 0)
    for ref in (first_state, total, arrived):
        ref[...] = jnp.zeros_like(ref)

    lanes = lax.broadcasted_iota(jnp.int32, (128, 128), 1)
    subs = lax.broadcasted_iota(jnp.int32, (128, 128), 0)
    eye = lanes == subs
    row_ids = lax.broadcasted_iota(jnp.int32, (ROWS, HD), 0)
    spots = row_ids + row_ids // PIECE * (SLOT - PIECE) - lax.broadcasted_iota(jnp.int32, (ROWS, HD), 1)
    ones_v = jnp.ones((BLOCK, HD), BF16)
    feats = heads * FEAT
    tail = jnp.where(lax.broadcasted_iota(jnp.int32, (128 - feats, tokens), 0) == 0, 1.0, 0.0).astype(BF16)
    fk[pl.ds(feats, 128 - feats), :] = tail
    fq[pl.ds(feats, 128 - feats), :] = tail
    for index in range(4):
        loads[index].wait()
    loads[4].wait()

    def put(ref, h, state):
        for piece in range(PIECES):
            ref[h * PIECES + piece, 0:PIECE, :] = state[piece * PIECE : (piece + 1) * PIECE]

    def state_of(h):
        cols = pl.ds(pl.multiple_of(h * HD, HD), HD)
        summed = None
        for block in range(blocks):
            keys = fk[:, pl.ds(block * BLOCK, BLOCK)]
            scale = sk[...]
            mapped = dot(ea[h], keys) * dot(eb[h], keys)
            mapped = (mapped * jnp.concatenate([scale] * (BLOCK // 128), axis=1)).astype(BF16)
            both = dot(mapped, jnp.concatenate([v[pl.ds(block * BLOCK, BLOCK), cols], ones_v], axis=1))
            state, normal = both[:, :HD], both[:, HD:]
            low = jnp.sum(jnp.where(spots == 0, normal, 0.0), axis=0, keepdims=True)
            high = jnp.sum(jnp.where(spots == HD, normal, 0.0), axis=0, keepdims=True)
            state = jnp.where(row_ids == normal_row, low, jnp.where(row_ids == normal_row + 1, high, state))
            if block == 0:
                put(first_state, h, state)
            summed = state if summed is None else summed + state
        put(total, h, summed)

    def states(start):
        def body(i, carry):
            state_of(start + i)
            return carry
        lax.fori_loop(0, half, body, 0, unroll=True)

    states(half * (1 - core))
    pl.semaphore_wait(barrier, 1 + 1 + head_n - 1 + chips - 1)
    swap_out = remote(total.at[pl.ds((1 - core) * pieces, pieces)], got, 0, other, head)
    swap_out.start()
    states(half * core)

    following = lax.rem(me + 1, seq_n)
    edges = [
        remote(wk_hbm.at[pl.ds(tokens - W, W)], edge_k, 1, following, head),
        remote(wv_hbm.at[pl.ds(tokens - W, W)], edge_v, 2, following, head),
    ]
    for copy in edges:
        copy.start()
    swap_out.wait_recv()
    own = pl.ds(core * pieces, pieces)
    chip_sum[...] = total[own] + got[...]

    def far_first(step):
        away = step // x_n
        along_z = lax.rem(z_n // 2 + jnp.where(lax.rem(away, 2) == 0, away // 2, z_n - (away + 1) // 2), z_n)
        x, z = chip // z_n, lax.rem(chip, z_n)
        return lax.rem(x + lax.rem(step, x_n), x_n) * z_n + lax.rem(z + along_z, z_n)

    def to_chips(src, dst, index):
        def send(step, carry):
            there = far_first(step)

            @pl.when(there != chip)
            def _():
                remote(
                    src.at[there, pl.ds(0, PIECE)], dst.at[chip, pl.ds(0, PIECE)], index, 2 * there + core, head
                ).start()
            return carry

        lax.fori_loop(0, chips, send, 0)
        dst[chip] = src[chip]

    to_chips(chip_sum, gathered, 3)

    for copy in loads[5:]:
        copy.wait()
    quarter = BLOCK // 2
    tri = lax.broadcasted_iota(jnp.int32, (quarter, quarter), 0) >= lax.broadcasted_iota(jnp.int32, (quarter, quarter), 1)
    feat_lane = lax.broadcasted_iota(jnp.int32, (1, 128), 1)
    fq_rows[...] = fq[...].T

    def within(i, carry):
        h, block = i // blocks, lax.rem(i, blocks)
        cols = pl.ds(pl.multiple_of(h * HD, HD), HD)
        start = pl.multiple_of(block * BLOCK, BLOCK)
        keys = fk[:, pl.ds(start, BLOCK)]
        mine = jnp.where(feat_lane // FEAT == h, 1.0, 0.0).astype(BF16)
        ext = fq_rows[pl.ds(start, BLOCK), :]
        queries = ext * mine
        vals = jnp.concatenate([v[pl.ds(start, BLOCK), cols], ones_v], axis=1)

        def weights(q, k):
            s = dot(q, k)
            return 1.0 + s * 0.25 + s * s * (1.0 / 32.0)

        top = jnp.where(tri, weights(queries[:quarter], keys[:, :quarter]), 0.0).astype(BF16)
        local[h, pl.ds(start, quarter), :] = dot(top, vals[:quarter])
        left = weights(queries[quarter:], keys[:, :quarter]).astype(BF16)
        right = jnp.where(tri, weights(queries[quarter:], keys[:, quarter:]), 0.0).astype(BF16)
        local[h, pl.ds(start + quarter, quarter), :] = dot(jnp.concatenate([left, right], axis=1), vals)
        mapped = dot_nt(ext, eaq[h]) * dot_nt(ext, ebq[h]) * sq[0:1, :]
        map_q[h, pl.ds(start, BLOCK), :] = mapped.astype(BF16)
        return carry

    lax.fori_loop(0, heads * blocks, within, 0, unroll=4)

    settle(gathered, chips - 1, recv_sem.at[3])

    def add(u, run):
        prefixes[u] = run
        return run + gathered[u]

    lax.fori_loop(0, chips, add, jnp.zeros((SLOT, HD), F32), unroll=8)
    to_chips(prefixes, arrived, 4)

    band_row = lax.broadcasted_iota(jnp.int32, (W, 2 * W), 0)
    band_col = lax.broadcasted_iota(jnp.int32, (W, 2 * W), 1)
    band = (band_col > band_row) & (band_col <= band_row + W)
    sharp = 1.0 / math.sqrt(HD)

    def attend(scores, allowed):
        scores = jnp.where(allowed, scores * sharp, -1e30)
        weights = jnp.exp(scores - jnp.max(scores, axis=1, keepdims=True))
        return (weights / jnp.sum(weights, axis=1, keepdims=True)).astype(BF16)

    group = 8
    band_group = jnp.concatenate([band] * group, axis=0)

    def windows(h, first, count):
        cols = pl.ds(pl.multiple_of(h * HD, HD), HD)
        starts = [first + c * W for c in range(count)]
        scores = [
            dot_nt(wq[pl.ds(s, W), cols], wk[pl.ds(s - W, 2 * W), cols]) for s in starts
        ]
        probs = attend(jnp.concatenate(scores, axis=0), band_group[: count * W])
        for c, s in enumerate(starts):
            window[pl.ds(s, W), cols] = dot(probs[c * W : (c + 1) * W], wv[pl.ds(s - W, 2 * W), cols])

    def window_head(h, carry):
        windows(h, W, group - 1)

        def rest(g, inner):
            windows(h, pl.multiple_of(g * group * W, group * W), group)
            return inner

        return lax.fori_loop(1, tokens // (group * W), rest, carry, unroll=True)

    lax.fori_loop(0, heads, window_head, 0)

    edges[0].wait_recv()
    edges[1].wait_recv()
    band_first = band & ((band_col >= W) | (me > 0))

    def window_edge(h, carry):
        cols = pl.ds(pl.multiple_of(h * HD, HD), HD)
        keys = jnp.concatenate([edge_k[:, cols], wk[pl.ds(0, W), cols]], axis=0)
        vals = jnp.concatenate([edge_v[:, cols], wv[pl.ds(0, W), cols]], axis=0)
        probs = attend(dot_nt(wq[pl.ds(0, W), cols], keys), band_first)
        window[pl.ds(0, W), cols] = dot(probs, vals)
        return carry

    lax.fori_loop(0, heads, window_edge, 0, unroll=True)

    settle(arrived, chips - 1, recv_sem.at[4])
    ahead = jnp.where(core == 0, 1.0, 0.0)
    payload[...] = arrived[...] + total[own] * ahead
    swap_back = remote(payload, before.at[own], 5, other, head)
    swap_back.start()
    before[own] = arrived[...] + got[...] * (1.0 - ahead)

    spot = normal_row // PIECE * SLOT + normal_row % PIECE

    def finish(h, block, fresh):
        cols = pl.ds(pl.multiple_of(h * HD, HD), HD)
        rows = pl.ds(block * BLOCK, BLOCK)
        mine = pl.ds(h * PIECES, PIECES)
        state = before[mine]
        if block > 0:
            state = state + first_state[mine]
        state = state.reshape(WIDE, HD)
        normal = jnp.concatenate(
            [jnp.broadcast_to(state[spot + i : spot + i + 1], (HD, HD)).T for i in range(2)], axis=0
        )
        high, low = split(jnp.concatenate([state, normal], axis=1))
        mapped = map_q[h, rows, :]
        sums = dot(mapped, high) + dot(mapped, low) + local[h, rows, :]
        combined = gain[h] * (sums[:, :HD] / sums[:, HD:] + window[rows, cols])
        window[rows, cols] = combined
        squared = combined * combined
        squares[rows, :] = squared if fresh else squares[rows, :] + squared

    own_head = half * core
    for block in range(blocks):
        finish(own_head, block, True)
    for i in range(1, half):
        for block in range(blocks):
            finish(own_head + i, block, False)
    swap_back.wait_recv()
    for block in range(blocks):
        for i in range(half):
            finish(half * (1 - core) + i, block, False)
        sums = jnp.sum(squares[pl.ds(block * BLOCK, BLOCK), :], axis=1, keepdims=True)
        for r in range(BLOCK // 128):
            wide = jnp.broadcast_to(sums[r * 128 : (r + 1) * 128], (128, 128))
            power_own[block, r : r + 1, :] = jnp.sum(jnp.where(eye, wide, 0.0), axis=0, keepdims=True)
        power_all[block, head] = power_own[block]
        for step in range(1, head_n):
            remote(
                power_own.at[block], power_all.at[block, head], 6 + block, me, lax.rem(head + step, head_n)
            ).start()

    for block in range(blocks):
        settle(power_all.at[block], head_n - 1, recv_sem.at[6 + block], BLOCK // 128)
        power = jnp.sum(power_all[block], axis=0) * (1.0 / (heads * head_n * HD))
        factor = lax.rsqrt(power + EPS)
        for r in range(BLOCK // 128):
            some = pl.ds(block * BLOCK + r * 128, 128)
            column = jnp.broadcast_to(factor[r : r + 1], (128, 128)).T
            out[some, :] = (window[some, :] * jnp.concatenate([column] * heads, axis=1)).astype(BF16)

    swap_out.wait_send()
    for copy in edges:
        copy.wait_send()
    swap_back.wait_send()

    settle(gathered, chips - 1, send_sem.at[3])
    settle(arrived, chips - 1, send_sem.at[4])
    for block in range(blocks):
        settle(power_all.at[block], head_n - 1, send_sem.at[6 + block], BLOCK // 128)


def solution(mesh):
    seq_n, head_n = mesh.shape["seq"], mesh.shape["head"]
    z_n = 8

    def local(feat_q, feat_k, values, win_q, win_k, win_v, head_gain):
        tokens, width = values.shape
        heads = head_gain.shape[0]
        *tables, normal_row = feature_tables(heads)
        chips = seq_n // 2
        pieces = heads // 2 * PIECES
        blocks = tokens // BLOCK
        dims = (seq_n, head_n, z_n, heads, tokens, normal_row)
        anywhere = pl.BlockSpec(memory_space=pltpu.HBM)
        vm = pltpu.VMEM
        stay = functools.partial(pltpu.with_memory_space_constraint, memory_space=pltpu.HBM)
        return pl.pallas_call(
            functools.partial(mixer, dims),
            out_shape=jax.ShapeDtypeStruct((tokens, width), BF16),
            in_specs=[anywhere] * 6 + [pl.BlockSpec(memory_space=pltpu.SMEM)] + [anywhere] * 6,
            out_specs=pl.BlockSpec(memory_space=pltpu.VMEM),
            scratch_shapes=[
                vm((128, tokens), BF16), vm((128, tokens), BF16),
                vm(values.shape, BF16), vm(values.shape, BF16), vm(values.shape, BF16), vm(values.shape, BF16),
                vm((heads, ROWS, 128), BF16), vm((heads, ROWS, 128), BF16),
                vm((heads, WIDE, 128), BF16), vm((heads, WIDE, 128), BF16), vm((ROWS, 128), F32), vm((8, WIDE), F32),
                vm((W, width), BF16), vm((W, width), BF16),
                vm((2 * pieces, SLOT, HD), F32),
                vm((2 * pieces, SLOT, HD), F32),
                vm((pieces, SLOT, HD), F32),
                vm((pieces, SLOT, HD), F32),
                vm((chips, SLOT, HD), F32),
                vm((chips, SLOT, HD), F32),
                vm((pieces, SLOT, HD), F32),
                vm((pieces, SLOT, HD), F32),
                vm((2 * pieces, SLOT, HD), F32),
                vm((tokens, 128), BF16),
                vm((heads, tokens, 2 * HD), F32),
                vm((tokens, width), F32),
                vm((heads, tokens, WIDE), BF16),
                vm((blocks, BLOCK // 128, 128), F32),
                vm((blocks, head_n, BLOCK // 128, 128), F32),
                vm((tokens, HD), F32),
                pltpu.SemaphoreType.DMA((12,)),
                pltpu.SemaphoreType.DMA((6 + blocks,)),
                pltpu.SemaphoreType.DMA((6 + blocks,)),
            ],
            compiler_params=pltpu.CompilerParams(
                collective_id=0, has_side_effects=True, vmem_limit_bytes=48 * 2**20
            ),
            name="mixer",
        )(
            *(stay(x) for x in (feat_q.T, feat_k.T, values, win_q, win_k, win_v, head_gain)),
            *(stay(x) for x in (
                *(jnp.asarray(table, BF16) for table in tables[:4]), *(jnp.asarray(table) for table in tables[4:]),
            )),
        )

    placed = (P("seq", "head"),) * 6 + (P("head"),)
    return jax.shard_map(local, mesh=mesh, in_specs=placed, out_specs=P("seq", "head"), check_vma=False)
```

```python
import functools
import math

import jax
import jax.numpy as jnp
import numpy as np
from jax import lax
from jax.experimental import pallas as pl
from jax.experimental.pallas import tpu as pltpu
from jax.sharding import PartitionSpec as P

MESH = pl.DeviceIdType.MESH
F32 = jnp.float32
BF16 = jnp.bfloat16

W = 64
BLOCK = 512
FEAT = 16
HD = 128
ROWS = 160
PIECE = 10
SLOT = 16
PIECES = ROWS // PIECE
WIDE = PIECES * SLOT
QUAD = 1.0 / (4.0 * math.sqrt(2.0))
EPS = 1e-06


def feature_tables(heads):
    ones_lane = heads * FEAT
    first = np.zeros((heads, ROWS, 128), np.float32)
    second = np.zeros((heads, ROWS, 128), np.float32)
    scale_k = np.zeros((ROWS,), np.float32)
    scale_q = np.zeros((ROWS,), np.float32)
    row = 0
    for shift in range(FEAT // 2 + 1):
        for a in range(FEAT if shift < FEAT // 2 else FEAT // 2):
            for h in range(heads):
                first[h, row, h * FEAT + a] = 1.0
                second[h, row, h * FEAT + (a + shift) % FEAT] = 1.0
            scale_k[row] = QUAD
            scale_q[row] = np.float32(QUAD) * (1.0 if shift == 0 else 2.0)
            row += 1
    for a in range(FEAT):
        for h in range(heads):
            first[h, row, h * FEAT + a] = 1.0
            second[h, row, ones_lane] = 1.0
        scale_k[row] = scale_q[row] = 0.5
        row += 1
    first[:, row, ones_lane] = 1.0
    second[:, row, ones_lane] = 1.0
    scale_k[row] = scale_q[row] = 1.0
    row += 1
    assert row + 2 <= ROWS
    spot = np.arange(ROWS) // PIECE * SLOT + np.arange(ROWS) % PIECE
    first_q = np.zeros((heads, WIDE, 128), np.float32)
    second_q = np.zeros((heads, WIDE, 128), np.float32)
    first_q[:, spot], second_q[:, spot] = first, second
    wide_k = np.ascontiguousarray(np.broadcast_to(scale_k[:, None], (ROWS, 128)))
    wide_q = np.zeros((8, WIDE), np.float32)
    wide_q[:, spot] = scale_q
    return first, second, first_q, second_q, wide_k, wide_q, row


def dot(a, b):
    return jnp.dot(a, b, preferred_element_type=F32)


def dot_nt(a, b):
    return lax.dot_general(a, b, (((1,), (1,)), ((), ())), preferred_element_type=F32)


def split(x):
    high = x.astype(BF16)
    return high, (x - high.astype(F32)).astype(BF16)


def mixer(
    dims,
    fq_hbm, fk_hbm, v_hbm, wq_hbm, wk_hbm, wv_hbm, gain, ea_hbm, eb_hbm, eaq_hbm, ebq_hbm, sk_hbm, sq_hbm,
    out,
    fq, fk, v, wq, wk, wv, ea, eb, eaq, ebq, sk, sq,
    edge_k, edge_v, first_state, total, got, chip_sum, gathered, prefixes, arrived, payload, before,
    fq_rows, local, window, map_q, power_own, power_all, squares,
    in_sem, send_sem, recv_sem,
):
    seq_n, head_n, z_n, heads, tokens, normal_row = dims
    x_n = seq_n // 2 // z_n
    chips = seq_n // 2
    half = heads // 2
    pieces = half * PIECES
    blocks = tokens // BLOCK
    me, head = lax.axis_index("seq"), lax.axis_index("head")
    core = lax.rem(me, 2)
    chip = me // 2
    other = me + 1 - 2 * core

    def load(index, src, dst):
        return pltpu.make_async_copy(src, dst, in_sem.at[index])

    first_loads = [load(0, fk_hbm, fk.at[pl.ds(0, heads * FEAT)]), load(1, ea_hbm, ea), load(2, eb_hbm, eb), load(3, sk_hbm, sk)]
    first_loads.append(load(4, v_hbm, v))
    later_loads = [
        load(5, fq_hbm, fq.at[pl.ds(0, heads * FEAT)]), load(6, sq_hbm, sq), load(10, eaq_hbm, eaq), load(11, ebq_hbm, ebq),
        load(7, wk_hbm, wk), load(8, wq_hbm, wq), load(9, wv_hbm, wv),
    ]

    def remote(src, dst, index, seq, group):
        return pltpu.make_async_remote_copy(
            src_ref=src, dst_ref=dst, send_sem=send_sem.at[index], recv_sem=recv_sem.at[index],
            device_id=(seq, group), device_id_type=MESH,
        )

    def settle(buffer, count, sem, rows=PIECE):
        part = buffer.at[pl.ds(0, count), pl.ds(0, rows)]
        pltpu.make_async_copy(part, part, sem).wait()

    barrier = pltpu.get_barrier_semaphore()
    edge_mate = lax.rem(me + 2 * core - 1 + seq_n, seq_n)

    def greet(seq, group):
        pl.semaphore_signal(barrier, inc=1, device_id=(seq, group), device_id_type=MESH)

    x, z = chip // z_n, lax.rem(chip, z_n)
    away = sorted(
        ((dx, dz) for dx in range(x_n) for dz in range(z_n) if dx or dz),
        key=lambda d: -(min(d[0], x_n - d[0]) + 1.01 * min(d[1], z_n - d[1])),
    )
    others = [lax.rem(x + dx, x_n) * z_n + lax.rem(z + dz, z_n) for dx, dz in away]
    for there in others:
        greet(2 * there + core, head)
    greet(other, head)
    greet(edge_mate, head)
    for step in range(1, head_n):
        greet(me, lax.rem(head + step, head_n))
    for copy in first_loads:
        copy.start()
    for ref in (first_state, total, arrived):
        ref[...] = jnp.zeros_like(ref)

    lanes = lax.broadcasted_iota(jnp.int32, (128, 128), 1)
    subs = lax.broadcasted_iota(jnp.int32, (128, 128), 0)
    eye = lanes == subs
    row_ids = lax.broadcasted_iota(jnp.int32, (ROWS, HD), 0)
    spots = row_ids + row_ids // PIECE * (SLOT - PIECE) - lax.broadcasted_iota(jnp.int32, (ROWS, HD), 1)
    ones_v = jnp.ones((BLOCK, HD), BF16)
    feats = heads * FEAT
    tail = jnp.where(lax.broadcasted_iota(jnp.int32, (128 - feats, tokens), 0) == 0, 1.0, 0.0).astype(BF16)
    fk[pl.ds(feats, 128 - feats), :] = tail
    fq[pl.ds(feats, 128 - feats), :] = tail
    for copy in first_loads:
        copy.wait()
    for copy in later_loads:
        copy.start()

    def put(ref, h, state):
        for piece in range(PIECES):
            ref[h * PIECES + piece, 0:PIECE, :] = state[piece * PIECE : (piece + 1) * PIECE]

    def state_of(h):
        cols = pl.ds(pl.multiple_of(h * HD, HD), HD)
        summed = None
        for block in range(blocks):
            keys = fk[:, pl.ds(block * BLOCK, BLOCK)]
            scale = sk[...]
            mapped = dot(ea[h], keys) * dot(eb[h], keys)
            mapped = (mapped * jnp.concatenate([scale] * (BLOCK // 128), axis=1)).astype(BF16)
            both = dot(mapped, jnp.concatenate([v[pl.ds(block * BLOCK, BLOCK), cols], ones_v], axis=1))
            state, normal = both[:, :HD], both[:, HD:]
            low = jnp.sum(jnp.where(spots == 0, normal, 0.0), axis=0, keepdims=True)
            high = jnp.sum(jnp.where(spots == HD, normal, 0.0), axis=0, keepdims=True)
            state = jnp.where(row_ids == normal_row, low, jnp.where(row_ids == normal_row + 1, high, state))
            if block == 0:
                put(first_state, h, state)
            summed = state if summed is None else summed + state
        put(total, h, summed)

    def states(start):
        def body(i, carry):
            state_of(start + i)
            return carry
        lax.fori_loop(0, half, body, 0, unroll=True)

    states(half * (1 - core))
    pl.semaphore_wait(barrier, 1 + 1 + head_n - 1 + chips - 1)
    swap_out = remote(total.at[pl.ds((1 - core) * pieces, pieces)], got, 0, other, head)
    swap_out.start()
    states(half * core)

    following = lax.rem(me + 1, seq_n)
    edges = [
        remote(wk_hbm.at[pl.ds(tokens - W, W)], edge_k, 1, following, head),
        remote(wv_hbm.at[pl.ds(tokens - W, W)], edge_v, 2, following, head),
    ]
    for copy in edges:
        copy.start()
    swap_out.wait_recv()
    own = pl.ds(core * pieces, pieces)
    chip_sum[...] = total[own] + got[...]

    def to_chips(src, dst, index):
        for there in others:
            remote(src.at[there, pl.ds(0, PIECE)], dst.at[chip, pl.ds(0, PIECE)], index, 2 * there + core, head).start()
        dst[chip] = src[chip]

    to_chips(chip_sum, gathered, 3)

    for copy in later_loads:
        copy.wait()
    quarter = BLOCK // 2
    tri = lax.broadcasted_iota(jnp.int32, (quarter, quarter), 0) >= lax.broadcasted_iota(jnp.int32, (quarter, quarter), 1)
    feat_lane = lax.broadcasted_iota(jnp.int32, (1, 128), 1)
    fq_rows[...] = fq[...].T

    def within(i, carry):
        h, block = i // blocks, lax.rem(i, blocks)
        cols = pl.ds(pl.multiple_of(h * HD, HD), HD)
        start = pl.multiple_of(block * BLOCK, BLOCK)
        keys = fk[:, pl.ds(start, BLOCK)]
        mine = jnp.where(feat_lane // FEAT == h, 1.0, 0.0).astype(BF16)
        ext = fq_rows[pl.ds(start, BLOCK), :]
        queries = ext * mine
        vals = jnp.concatenate([v[pl.ds(start, BLOCK), cols], ones_v], axis=1)

        def weights(q, k):
            s = dot(q, k)
            return 1.0 + s * 0.25 + s * s * (1.0 / 32.0)

        top = jnp.where(tri, weights(queries[:quarter], keys[:, :quarter]), 0.0).astype(BF16)
        local[h, pl.ds(start, quarter), :] = dot(top, vals[:quarter])
        left = weights(queries[quarter:], keys[:, :quarter]).astype(BF16)
        right = jnp.where(tri, weights(queries[quarter:], keys[:, quarter:]), 0.0).astype(BF16)
        local[h, pl.ds(start + quarter, quarter), :] = dot(jnp.concatenate([left, right], axis=1), vals)
        mapped = dot_nt(ext, eaq[h]) * dot_nt(ext, ebq[h]) * sq[0:1, :]
        map_q[h, pl.ds(start, BLOCK), :] = mapped.astype(BF16)
        return carry

    lax.fori_loop(0, heads * blocks, within, 0, unroll=4)

    spot = normal_row // PIECE * SLOT + normal_row % PIECE

    def state_halves(ref, h):
        state = ref[pl.ds(h * PIECES, PIECES)].reshape(WIDE, HD)
        normal = jnp.concatenate(
            [jnp.broadcast_to(state[spot + i : spot + i + 1], (HD, HD)).T for i in range(2)], axis=0
        )
        return split(jnp.concatenate([state, normal], axis=1))

    def apply_state(mapped, halves):
        return dot(mapped, halves[0]) + dot(mapped, halves[1])

    def first_block(h, carry):
        rows = pl.ds(BLOCK, BLOCK)
        local[h, rows, :] += apply_state(map_q[h, rows, :], state_halves(first_state, h))
        return carry

    lax.fori_loop(0, heads, first_block, 0, unroll=2)

    band_row = lax.broadcasted_iota(jnp.int32, (W, 2 * W), 0)
    band_col = lax.broadcasted_iota(jnp.int32, (W, 2 * W), 1)
    band = (band_col > band_row) & (band_col <= band_row + W)
    sharp = 1.0 / math.sqrt(HD)

    def attend(scores, allowed):
        scores = jnp.where(allowed, scores * sharp, -1e30)
        weights = jnp.exp(scores - jnp.max(scores, axis=1, keepdims=True))
        return (weights / jnp.sum(weights, axis=1, keepdims=True)).astype(BF16)

    group = 8
    band_group = jnp.concatenate([band] * group, axis=0)

    def windows(h, first, count):
        cols = pl.ds(pl.multiple_of(h * HD, HD), HD)
        starts = [first + c * W for c in range(count)]
        scores = [
            dot_nt(wq[pl.ds(s, W), cols], wk[pl.ds(s - W, 2 * W), cols]) for s in starts
        ]
        probs = attend(jnp.concatenate(scores, axis=0), band_group[: count * W])
        for c, s in enumerate(starts):
            window[pl.ds(s, W), cols] = dot(probs[c * W : (c + 1) * W], wv[pl.ds(s - W, 2 * W), cols])

    def window_head(h, carry):
        windows(h, W, group - 1)

        def rest(g, inner):
            windows(h, pl.multiple_of(g * group * W, group * W), group)
            return inner

        return lax.fori_loop(1, tokens // (group * W), rest, carry, unroll=True)

    lax.fori_loop(0, half, window_head, 0)

    settle(gathered, chips - 1, recv_sem.at[3])

    def add(u, run):
        prefixes[u] = run
        return run + gathered[u]

    lax.fori_loop(0, chips, add, jnp.zeros((SLOT, HD), F32), unroll=8)
    to_chips(prefixes, arrived, 4)

    lax.fori_loop(half, heads, window_head, 0)

    edges[0].wait_recv()
    edges[1].wait_recv()
    band_first = band & ((band_col >= W) | (me > 0))

    def window_edge(h, carry):
        cols = pl.ds(pl.multiple_of(h * HD, HD), HD)
        keys = jnp.concatenate([edge_k[:, cols], wk[pl.ds(0, W), cols]], axis=0)
        vals = jnp.concatenate([edge_v[:, cols], wv[pl.ds(0, W), cols]], axis=0)
        probs = attend(dot_nt(wq[pl.ds(0, W), cols], keys), band_first)
        window[pl.ds(0, W), cols] = dot(probs, vals)
        return carry

    lax.fori_loop(0, heads, window_edge, 0, unroll=True)

    ahead = jnp.where(core == 0, 1.0, 0.0)

    @pl.when(chip > 0)
    def _():
        settle(arrived, chips - 1, recv_sem.at[4])
        payload[...] = arrived[...] + total[own] * ahead
        before[own] = arrived[...] + got[...] * (1.0 - ahead)

    @pl.when(chip == 0)
    def _():
        payload[...] = total[own] * ahead
        before[own] = got[...] * (1.0 - ahead)

    swap_back = remote(payload, before.at[pl.ds(core * pieces, pieces)], 5, other, head)
    swap_back.start()

    def finish(h, block, halves, fresh):
        cols = pl.ds(pl.multiple_of(h * HD, HD), HD)
        rows = pl.ds(block * BLOCK, BLOCK)
        sums = apply_state(map_q[h, rows, :], halves) + local[h, rows, :]
        combined = gain[h] * (sums[:, :HD] / sums[:, HD:] + window[rows, cols])
        window[rows, cols] = combined
        squared = combined * combined
        squares[rows, :] = squared if fresh else squares[rows, :] + squared

    for i in range(half):
        h = half * core + i
        halves = state_halves(before, h)
        for block in range(blocks):
            finish(h, block, halves, i == 0)
    swap_back.wait_recv()
    rest = [half * (1 - core) + i for i in range(half)]
    rest_halves = [state_halves(before, h) for h in rest]
    for block in range(blocks):
        for h, halves in zip(rest, rest_halves):
            finish(h, block, halves, False)
        sums = jnp.sum(squares[pl.ds(block * BLOCK, BLOCK), :], axis=1, keepdims=True)
        for r in range(BLOCK // 128):
            wide = jnp.broadcast_to(sums[r * 128 : (r + 1) * 128], (128, 128))
            power_own[block, r : r + 1, :] = jnp.sum(jnp.where(eye, wide, 0.0), axis=0, keepdims=True)
        power_all[block, head] = power_own[block]
        for step in range(1, head_n):
            remote(
                power_own.at[block], power_all.at[block, head], 6 + block, me, lax.rem(head + step, head_n)
            ).start()

    for block in range(blocks):
        settle(power_all.at[block], head_n - 1, recv_sem.at[6 + block], BLOCK // 128)
        power = jnp.sum(power_all[block], axis=0) * (1.0 / (heads * head_n * HD))
        factor = lax.rsqrt(power + EPS)
        for r in range(BLOCK // 128):
            some = pl.ds(block * BLOCK + r * 128, 128)
            column = jnp.broadcast_to(factor[r : r + 1], (128, 128)).T
            out[some, :] = (window[some, :] * jnp.concatenate([column] * heads, axis=1)).astype(BF16)

    @pl.when(chip == 0)
    def _():
        settle(arrived, chips - 1, recv_sem.at[4])

    swap_out.wait_send()
    for copy in edges:
        copy.wait_send()
    swap_back.wait_send()

    settle(gathered, chips - 1, send_sem.at[3])
    settle(arrived, chips - 1, send_sem.at[4])
    for block in range(blocks):
        settle(power_all.at[block], head_n - 1, send_sem.at[6 + block], BLOCK // 128)


def solution(mesh):
    seq_n, head_n = mesh.shape["seq"], mesh.shape["head"]
    z_n = 8

    def local(feat_q, feat_k, values, win_q, win_k, win_v, head_gain):
        tokens, width = values.shape
        heads = head_gain.shape[0]
        *tables, normal_row = feature_tables(heads)
        chips = seq_n // 2
        pieces = heads // 2 * PIECES
        blocks = tokens // BLOCK
        dims = (seq_n, head_n, z_n, heads, tokens, normal_row)
        anywhere = pl.BlockSpec(memory_space=pltpu.HBM)
        vm = pltpu.VMEM
        stay = functools.partial(pltpu.with_memory_space_constraint, memory_space=pltpu.HBM)
        return pl.pallas_call(
            functools.partial(mixer, dims),
            out_shape=jax.ShapeDtypeStruct((tokens, width), BF16),
            in_specs=[anywhere] * 6 + [pl.BlockSpec(memory_space=pltpu.SMEM)] + [anywhere] * 6,
            out_specs=pl.BlockSpec(memory_space=pltpu.VMEM),
            scratch_shapes=[
                vm((128, tokens), BF16), vm((128, tokens), BF16),
                vm(values.shape, BF16), vm(values.shape, BF16), vm(values.shape, BF16), vm(values.shape, BF16),
                vm((heads, ROWS, 128), BF16), vm((heads, ROWS, 128), BF16),
                vm((heads, WIDE, 128), BF16), vm((heads, WIDE, 128), BF16), vm((ROWS, 128), F32), vm((8, WIDE), F32),
                vm((W, width), BF16), vm((W, width), BF16),
                vm((2 * pieces, SLOT, HD), F32),
                vm((2 * pieces, SLOT, HD), F32),
                vm((pieces, SLOT, HD), F32),
                vm((pieces, SLOT, HD), F32),
                vm((chips, SLOT, HD), F32),
                vm((chips, SLOT, HD), F32),
                vm((pieces, SLOT, HD), F32),
                vm((pieces, SLOT, HD), F32),
                vm((2 * pieces, SLOT, HD), F32),
                vm((tokens, 128), BF16),
                vm((heads, tokens, 2 * HD), F32),
                vm((tokens, width), F32),
                vm((heads, tokens, WIDE), BF16),
                vm((blocks, BLOCK // 128, 128), F32),
                vm((blocks, head_n, BLOCK // 128, 128), F32),
                vm((tokens, HD), F32),
                pltpu.SemaphoreType.DMA((12,)),
                pltpu.SemaphoreType.DMA((6 + blocks,)),
                pltpu.SemaphoreType.DMA((6 + blocks,)),
            ],
            compiler_params=pltpu.CompilerParams(
                collective_id=0, has_side_effects=True, vmem_limit_bytes=48 * 2**20
            ),
            name="mixer",
        )(
            *(stay(x) for x in (feat_q.T, feat_k.T, values, win_q, win_k, win_v, head_gain)),
            *(stay(x) for x in (
                *(jnp.asarray(table, BF16) for table in tables[:4]), *(jnp.asarray(table) for table in tables[4:]),
            )),
        )

    placed = (P("seq", "head"),) * 6 + (P("head"),)
    return jax.shard_map(local, mesh=mesh, in_specs=placed, out_specs=P("seq", "head"), check_vma=False)
```

```python
import functools
import math

import jax
import jax.numpy as jnp
import numpy as np
from jax import lax
from jax.experimental import pallas as pl
from jax.experimental.pallas import tpu as pltpu
from jax.sharding import PartitionSpec as P

MESH = pl.DeviceIdType.MESH
F32 = jnp.float32
BF16 = jnp.bfloat16

W = 64
BLOCK = 512
FEAT = 16
HD = 128
ROWS = 160
PIECE = 10
SLOT = 16
PIECES = ROWS // PIECE
WIDE = PIECES * SLOT
QUAD = 1.0 / (4.0 * math.sqrt(2.0))
EPS = 1e-06


def feature_tables(heads):
    ones_lane = heads * FEAT
    first = np.zeros((heads, ROWS, 128), np.float32)
    second = np.zeros((heads, ROWS, 128), np.float32)
    scale_k = np.zeros((ROWS,), np.float32)
    scale_q = np.zeros((ROWS,), np.float32)
    row = 0
    for shift in range(FEAT // 2 + 1):
        for a in range(FEAT if shift < FEAT // 2 else FEAT // 2):
            for h in range(heads):
                first[h, row, h * FEAT + a] = 1.0
                second[h, row, h * FEAT + (a + shift) % FEAT] = 1.0
            scale_k[row] = QUAD
            scale_q[row] = np.float32(QUAD) * (1.0 if shift == 0 else 2.0)
            row += 1
    for a in range(FEAT):
        for h in range(heads):
            first[h, row, h * FEAT + a] = 1.0
            second[h, row, ones_lane] = 1.0
        scale_k[row] = scale_q[row] = 0.5
        row += 1
    first[:, row, ones_lane] = 1.0
    second[:, row, ones_lane] = 1.0
    scale_k[row] = scale_q[row] = 1.0
    row += 1
    assert row + 2 <= ROWS
    spot = np.arange(ROWS) // PIECE * SLOT + np.arange(ROWS) % PIECE
    first_q = np.zeros((heads, WIDE, 128), np.float32)
    second_q = np.zeros((heads, WIDE, 128), np.float32)
    first_q[:, spot], second_q[:, spot] = first, second
    wide_k = np.ascontiguousarray(np.broadcast_to(scale_k[:, None], (ROWS, 128)))
    wide_q = np.zeros((8, WIDE), np.float32)
    wide_q[:, spot] = scale_q
    return first, second, first_q, second_q, wide_k, wide_q, row


def dot(a, b):
    return jnp.dot(a, b, preferred_element_type=F32)


def dot_nt(a, b):
    return lax.dot_general(a, b, (((1,), (1,)), ((), ())), preferred_element_type=F32)


def split(x):
    high = x.astype(BF16)
    return high, (x - high.astype(F32)).astype(BF16)


def mixer(
    dims,
    fq_hbm, fk_hbm, v_hbm, wq_hbm, wk_hbm, wv_hbm, gain, ea_hbm, eb_hbm, eaq_hbm, ebq_hbm, sk_hbm, sq_hbm,
    out,
    fq, fk, v, wq, wk, wv, ea, eb, eaq, ebq, sk, sq,
    edge_k, edge_v, first_state, total, got, chip_sum, gathered, prefixes, arrived, payload, before,
    fq_rows, local, window, map_q, power_own, power_all, squares,
    in_sem, send_sem, recv_sem,
):
    seq_n, head_n, z_n, heads, tokens, normal_row = dims
    x_n = seq_n // 2 // z_n
    chips = seq_n // 2
    half = heads // 2
    pieces = half * PIECES
    blocks = tokens // BLOCK
    me, head = lax.axis_index("seq"), lax.axis_index("head")
    core = lax.rem(me, 2)
    chip = me // 2
    other = me + 1 - 2 * core

    def load(index, src, dst):
        return pltpu.make_async_copy(src, dst, in_sem.at[index])

    first_loads = [load(0, fk_hbm, fk.at[pl.ds(0, heads * FEAT)]), load(1, ea_hbm, ea), load(2, eb_hbm, eb), load(3, sk_hbm, sk)]
    first_loads.append(load(4, v_hbm, v))
    later_loads = [
        load(5, fq_hbm, fq.at[pl.ds(0, heads * FEAT)]), load(6, sq_hbm, sq), load(10, eaq_hbm, eaq), load(11, ebq_hbm, ebq),
        load(7, wk_hbm, wk), load(8, wq_hbm, wq), load(9, wv_hbm, wv),
    ]

    def remote(src, dst, index, seq, group):
        return pltpu.make_async_remote_copy(
            src_ref=src, dst_ref=dst, send_sem=send_sem.at[index], recv_sem=recv_sem.at[index],
            device_id=(seq, group), device_id_type=MESH,
        )

    def settle(buffer, count, sem, rows=PIECE):
        part = buffer.at[pl.ds(0, count), pl.ds(0, rows)]
        pltpu.make_async_copy(part, part, sem).wait()

    barrier = pltpu.get_barrier_semaphore()
    edge_mate = lax.rem(me + 2 * core - 1 + seq_n, seq_n)

    def greet(seq, group):
        pl.semaphore_signal(barrier, inc=1, device_id=(seq, group), device_id_type=MESH)

    for copy in first_loads:
        copy.start()
    for ref in (got, before, arrived):
        ref[...] = jnp.zeros_like(ref)
    x, z = chip // z_n, lax.rem(chip, z_n)
    away = sorted(
        ((dx, dz) for dx in range(x_n) for dz in range(z_n) if dx or dz),
        key=lambda d: -(min(d[0], x_n - d[0]) + 1.01 * min(d[1], z_n - d[1])),
    )
    others = [lax.rem(x + dx, x_n) * z_n + lax.rem(z + dz, z_n) for dx, dz in away]
    for there in others:
        greet(2 * there + core, head)
    greet(other, head)
    greet(edge_mate, head)
    for step in range(1, head_n):
        greet(me, lax.rem(head + step, head_n))
    for ref in (first_state, total):
        ref[...] = jnp.zeros_like(ref)

    row_ids = lax.broadcasted_iota(jnp.int32, (ROWS, HD), 0)
    spots = row_ids + row_ids // PIECE * (SLOT - PIECE) - lax.broadcasted_iota(jnp.int32, (ROWS, HD), 1)
    ones_v = jnp.ones((BLOCK, HD), BF16)
    feats = heads * FEAT
    tail = jnp.where(lax.broadcasted_iota(jnp.int32, (128 - feats, tokens), 0) == 0, 1.0, 0.0).astype(BF16)
    fk[pl.ds(feats, 128 - feats), :] = tail
    fq[pl.ds(feats, 128 - feats), :] = tail
    for copy in first_loads:
        copy.wait()
    for copy in later_loads:
        copy.start()

    def put(ref, h, state):
        for piece in range(PIECES):
            ref[h * PIECES + piece, 0:PIECE, :] = state[piece * PIECE : (piece + 1) * PIECE]

    def state_of(h):
        cols = pl.ds(pl.multiple_of(h * HD, HD), HD)
        summed = None
        for block in range(blocks):
            keys = fk[:, pl.ds(block * BLOCK, BLOCK)]
            scale = sk[...]
            mapped = dot(ea[h], keys) * dot(eb[h], keys)
            mapped = (mapped * jnp.concatenate([scale] * (BLOCK // 128), axis=1)).astype(BF16)
            both = dot(mapped, jnp.concatenate([v[pl.ds(block * BLOCK, BLOCK), cols], ones_v], axis=1))
            state, normal = both[:, :HD], both[:, HD:]
            low = jnp.sum(jnp.where(spots == 0, normal, 0.0), axis=0, keepdims=True)
            high = jnp.sum(jnp.where(spots == HD, normal, 0.0), axis=0, keepdims=True)
            state = jnp.where(row_ids == normal_row, low, jnp.where(row_ids == normal_row + 1, high, state))
            if block == 0:
                put(first_state, h, state)
            summed = state if summed is None else summed + state
        put(total, h, summed)

    def states(start):
        def body(i, carry):
            state_of(start + i)
            return carry
        lax.fori_loop(0, half, body, 0, unroll=True)

    states(half * (1 - core))
    pl.semaphore_wait(barrier, 1 + 1 + head_n - 1 + chips - 1)
    swap_out = remote(total.at[pl.ds((1 - core) * pieces, pieces), pl.ds(0, PIECE)], got.at[:, pl.ds(0, PIECE)], 0, other, head)
    swap_out.start()
    states(half * core)

    following = lax.rem(me + 1, seq_n)
    edges = [
        remote(wk_hbm.at[pl.ds(tokens - W, W)], edge_k, 1, following, head),
        remote(wv_hbm.at[pl.ds(tokens - W, W)], edge_v, 2, following, head),
    ]
    for copy in edges:
        copy.start()
    swap_out.wait_recv()
    own = pl.ds(core * pieces, pieces)
    chip_sum[...] = total[own] + got[...]

    def to_chips(src, dst, index):
        for there in others:
            remote(src.at[there, pl.ds(0, PIECE)], dst.at[chip, pl.ds(0, PIECE)], index, 2 * there + core, head).start()
        dst[chip] = src[chip]

    to_chips(chip_sum, gathered, 3)

    for copy in later_loads:
        copy.wait()
    quarter = BLOCK // 2
    tri = lax.broadcasted_iota(jnp.int32, (quarter, quarter), 0) >= lax.broadcasted_iota(jnp.int32, (quarter, quarter), 1)
    feat_lane = lax.broadcasted_iota(jnp.int32, (1, 128), 1)
    fq_rows[...] = fq[...].T

    def within(i, carry):
        h, block = i // blocks, lax.rem(i, blocks)
        cols = pl.ds(pl.multiple_of(h * HD, HD), HD)
        start = pl.multiple_of(block * BLOCK, BLOCK)
        keys = fk[:, pl.ds(start, BLOCK)]
        mine = jnp.where(feat_lane // FEAT == h, 1.0, 0.0).astype(BF16)
        ext = fq_rows[pl.ds(start, BLOCK), :]
        queries = ext * mine
        vals = jnp.concatenate([v[pl.ds(start, BLOCK), cols], ones_v], axis=1)

        def weights(q, k):
            s = dot(q, k)
            return 1.0 + s * 0.25 + s * s * (1.0 / 32.0)

        top = jnp.where(tri, weights(queries[:quarter], keys[:, :quarter]), 0.0).astype(BF16)
        local[h, pl.ds(start, quarter), :] = dot(top, vals[:quarter])
        left = weights(queries[quarter:], keys[:, :quarter]).astype(BF16)
        right = jnp.where(tri, weights(queries[quarter:], keys[:, quarter:]), 0.0).astype(BF16)
        local[h, pl.ds(start + quarter, quarter), :] = dot(jnp.concatenate([left, right], axis=1), vals)
        mapped = dot_nt(ext, eaq[h]) * dot_nt(ext, ebq[h]) * sq[0:1, :]
        map_q[h, pl.ds(start, BLOCK), :] = mapped.astype(BF16)
        return carry

    lax.fori_loop(0, heads * blocks, within, 0, unroll=4)

    spot = normal_row // PIECE * SLOT + normal_row % PIECE

    def state_halves(ref, h):
        state = ref[pl.ds(h * PIECES, PIECES)].reshape(WIDE, HD)
        normal = jnp.concatenate(
            [jnp.broadcast_to(state[spot + i : spot + i + 1], (HD, HD)) for i in range(2)], axis=1
        )
        return jnp.concatenate(split(state), axis=1), jnp.concatenate(split(normal), axis=0)

    def apply_state(mapped, halves):
        upper, lower = dot(mapped, halves[0]), dot_nt(mapped, halves[1])
        return jnp.concatenate([upper[:, :HD] + upper[:, HD:], lower[:, :HD] + lower[:, HD:]], axis=1)

    def first_block(h, carry):
        rows = pl.ds(BLOCK, BLOCK)
        local[h, rows, :] += apply_state(map_q[h, rows, :], state_halves(first_state, h))
        return carry

    lax.fori_loop(0, heads, first_block, 0, unroll=2)

    band_row = lax.broadcasted_iota(jnp.int32, (W, 2 * W), 0)
    band_col = lax.broadcasted_iota(jnp.int32, (W, 2 * W), 1)
    band = (band_col > band_row) & (band_col <= band_row + W)
    sharp = 1.0 / math.sqrt(HD)

    def attend(scores, allowed):
        scores = jnp.where(allowed, scores * sharp, -1e30)
        weights = jnp.exp(scores - jnp.max(scores, axis=1, keepdims=True))
        return (weights / jnp.sum(weights, axis=1, keepdims=True)).astype(BF16)

    group = 8
    band_group = jnp.concatenate([band] * group, axis=0)

    def windows(h, first, count):
        cols = pl.ds(pl.multiple_of(h * HD, HD), HD)
        starts = [first + c * W for c in range(count)]
        scores = [
            dot_nt(wq[pl.ds(s, W), cols], wk[pl.ds(s - W, 2 * W), cols]) for s in starts
        ]
        probs = attend(jnp.concatenate(scores, axis=0), band_group[: count * W])
        for c, s in enumerate(starts):
            window[pl.ds(s, W), cols] = dot(probs[c * W : (c + 1) * W], wv[pl.ds(s - W, 2 * W), cols])

    def window_head(h, carry):
        windows(h, W, group - 1)

        def rest(g, inner):
            windows(h, pl.multiple_of(g * group * W, group * W), group)
            return inner

        return lax.fori_loop(1, tokens // (group * W), rest, carry, unroll=True)

    settle(gathered, chips - 1, recv_sem.at[3])

    def add(u, run):
        prefixes[u] = run
        return run + gathered[u]

    lax.fori_loop(0, chips, add, jnp.zeros((SLOT, HD), F32), unroll=8)
    to_chips(prefixes, arrived, 4)

    lax.fori_loop(0, heads, window_head, 0)

    edges[0].wait_recv()
    edges[1].wait_recv()
    band_first = band & ((band_col >= W) | (me > 0))

    def window_edge(h, carry):
        cols = pl.ds(pl.multiple_of(h * HD, HD), HD)
        keys = jnp.concatenate([edge_k[:, cols], wk[pl.ds(0, W), cols]], axis=0)
        vals = jnp.concatenate([edge_v[:, cols], wv[pl.ds(0, W), cols]], axis=0)
        probs = attend(dot_nt(wq[pl.ds(0, W), cols], keys), band_first)
        window[pl.ds(0, W), cols] = dot(probs, vals)
        return carry

    lax.fori_loop(0, heads, window_edge, 0, unroll=True)

    ahead = jnp.where(core == 0, 1.0, 0.0)

    @pl.when(chip > 0)
    def _():
        settle(arrived, chips - 1, recv_sem.at[4])
        payload[...] = arrived[...] + total[own] * ahead
        before[own] = arrived[...] + got[...] * (1.0 - ahead)

    @pl.when(chip == 0)
    def _():
        payload[...] = total[own] * ahead
        before[own] = got[...] * (1.0 - ahead)

    swap_back = remote(payload.at[:, pl.ds(0, PIECE)], before.at[pl.ds(core * pieces, pieces), pl.ds(0, PIECE)], 5, other, head)
    swap_back.start()

    def finish(h, block, halves, fresh):
        cols = pl.ds(pl.multiple_of(h * HD, HD), HD)
        rows = pl.ds(block * BLOCK, BLOCK)
        sums = apply_state(map_q[h, rows, :], halves) + local[h, rows, :]
        combined = gain[h] * (sums[:, :HD] / sums[:, HD:] + window[rows, cols])
        window[rows, cols] = combined
        squared = combined * combined
        squares[rows, :] = squared if fresh else squares[rows, :] + squared

    for i in range(half):
        h = half * core + i
        halves = state_halves(before, h)
        for block in range(blocks):
            finish(h, block, halves, i == 0)
    swap_back.wait_recv()
    rest = [half * (1 - core) + i for i in range(half)]
    rest_halves = [state_halves(before, h) for h in rest]
    for block in range(blocks):
        for h, halves in zip(rest, rest_halves):
            finish(h, block, halves, False)
        for r in range(BLOCK // 128):
            turned = squares[pl.ds(block * BLOCK + r * 128, 128), :].T
            power_own[block, r : r + 1, :] = jnp.sum(turned, axis=0, keepdims=True)
        power_all[block, head] = power_own[block]
        for step in range(1, head_n):
            remote(
                power_own.at[block], power_all.at[block, head], 6 + block, me, lax.rem(head + step, head_n)
            ).start()

    for block in range(blocks):
        settle(power_all.at[block], head_n - 1, recv_sem.at[6 + block], BLOCK // 128)
        power = jnp.sum(power_all[block], axis=0) * (1.0 / (heads * head_n * HD))
        factor = lax.rsqrt(power + EPS)
        for r in range(BLOCK // 128):
            some = pl.ds(block * BLOCK + r * 128, 128)
            column = jnp.broadcast_to(factor[r : r + 1], (128, 128)).T
            out[some, :] = (window[some, :] * jnp.concatenate([column] * heads, axis=1)).astype(BF16)

    @pl.when(chip == 0)
    def _():
        settle(arrived, chips - 1, recv_sem.at[4])

    swap_out.wait_send()
    for copy in edges:
        copy.wait_send()
    swap_back.wait_send()

    settle(gathered, chips - 1, send_sem.at[3])
    settle(arrived, chips - 1, send_sem.at[4])
    for block in range(blocks):
        settle(power_all.at[block], head_n - 1, send_sem.at[6 + block], BLOCK // 128)


def solution(mesh):
    seq_n, head_n = mesh.shape["seq"], mesh.shape["head"]
    z_n = 8

    def local(feat_q, feat_k, values, win_q, win_k, win_v, head_gain):
        tokens, width = values.shape
        heads = head_gain.shape[0]
        *tables, normal_row = feature_tables(heads)
        chips = seq_n // 2
        pieces = heads // 2 * PIECES
        blocks = tokens // BLOCK
        dims = (seq_n, head_n, z_n, heads, tokens, normal_row)
        anywhere = pl.BlockSpec(memory_space=pltpu.HBM)
        vm = pltpu.VMEM
        stay = functools.partial(pltpu.with_memory_space_constraint, memory_space=pltpu.HBM)
        return pl.pallas_call(
            functools.partial(mixer, dims),
            out_shape=jax.ShapeDtypeStruct((tokens, width), BF16),
            in_specs=[anywhere] * 6 + [pl.BlockSpec(memory_space=pltpu.SMEM)] + [anywhere] * 6,
            out_specs=pl.BlockSpec(memory_space=pltpu.VMEM),
            scratch_shapes=[
                vm((128, tokens), BF16), vm((128, tokens), BF16),
                vm(values.shape, BF16), vm(values.shape, BF16), vm(values.shape, BF16), vm(values.shape, BF16),
                vm((heads, ROWS, 128), BF16), vm((heads, ROWS, 128), BF16),
                vm((heads, WIDE, 128), BF16), vm((heads, WIDE, 128), BF16), vm((ROWS, 128), F32), vm((8, WIDE), F32),
                vm((W, width), BF16), vm((W, width), BF16),
                vm((2 * pieces, SLOT, HD), F32),
                vm((2 * pieces, SLOT, HD), F32),
                vm((pieces, SLOT, HD), F32),
                vm((pieces, SLOT, HD), F32),
                vm((chips, SLOT, HD), F32),
                vm((chips, SLOT, HD), F32),
                vm((pieces, SLOT, HD), F32),
                vm((pieces, SLOT, HD), F32),
                vm((2 * pieces, SLOT, HD), F32),
                vm((tokens, 128), BF16),
                vm((heads, tokens, 2 * HD), F32),
                vm((tokens, width), F32),
                vm((heads, tokens, WIDE), BF16),
                vm((blocks, BLOCK // 128, 128), F32),
                vm((blocks, head_n, BLOCK // 128, 128), F32),
                vm((tokens, HD), F32),
                pltpu.SemaphoreType.DMA((12,)),
                pltpu.SemaphoreType.DMA((6 + blocks,)),
                pltpu.SemaphoreType.DMA((6 + blocks,)),
            ],
            compiler_params=pltpu.CompilerParams(
                collective_id=0, has_side_effects=True, vmem_limit_bytes=48 * 2**20
            ),
            name="mixer",
        )(
            *(stay(x) for x in (feat_q.T, feat_k.T, values, win_q, win_k, win_v, head_gain)),
            *(stay(x) for x in (
                *(jnp.asarray(table, BF16) for table in tables[:4]), *(jnp.asarray(table) for table in tables[4:]),
            )),
        )

    placed = (P("seq", "head"),) * 6 + (P("head"),)
    return jax.shard_map(local, mesh=mesh, in_specs=placed, out_specs=P("seq", "head"), check_vma=False)
```

```python
import functools
import math

import jax
import jax.numpy as jnp
import numpy as np
from jax import lax
from jax.experimental import pallas as pl
from jax.experimental.pallas import tpu as pltpu
from jax.sharding import PartitionSpec as P

MESH = pl.DeviceIdType.MESH
F32 = jnp.float32
BF16 = jnp.bfloat16

W = 64
BLOCK = 512
FEAT = 16
HD = 128
ROWS = 160
PIECE = 10
SLOT = 16
PIECES = ROWS // PIECE
WIDE = PIECES * SLOT
QUAD = 1.0 / (4.0 * math.sqrt(2.0))
EPS = 1e-06


def feature_tables(heads):
    ones_lane = heads * FEAT
    first = np.zeros((heads, ROWS, 128), np.float32)
    second = np.zeros((heads, ROWS, 128), np.float32)
    scale_k = np.zeros((ROWS,), np.float32)
    scale_q = np.zeros((ROWS,), np.float32)
    row = 0
    for shift in range(FEAT // 2 + 1):
        for a in range(FEAT if shift < FEAT // 2 else FEAT // 2):
            for h in range(heads):
                first[h, row, h * FEAT + a] = 1.0
                second[h, row, h * FEAT + (a + shift) % FEAT] = 1.0
            scale_k[row] = QUAD
            scale_q[row] = np.float32(QUAD) * (1.0 if shift == 0 else 2.0)
            row += 1
    for a in range(FEAT):
        for h in range(heads):
            first[h, row, h * FEAT + a] = 1.0
            second[h, row, ones_lane] = 1.0
        scale_k[row] = scale_q[row] = 0.5
        row += 1
    first[:, row, ones_lane] = 1.0
    second[:, row, ones_lane] = 1.0
    scale_k[row] = scale_q[row] = 1.0
    row += 1
    assert row + 2 <= ROWS
    spot = np.arange(ROWS) // PIECE * SLOT + np.arange(ROWS) % PIECE
    first_q = np.zeros((heads, WIDE, 128), np.float32)
    second_q = np.zeros((heads, WIDE, 128), np.float32)
    first_q[:, spot], second_q[:, spot] = first, second
    wide_k = np.ascontiguousarray(np.broadcast_to(scale_k[:, None], (ROWS, 128)))
    wide_q = np.zeros((8, WIDE), np.float32)
    wide_q[:, spot] = scale_q
    return first, second, first_q, second_q, wide_k, wide_q, row


def dot(a, b):
    return jnp.dot(a, b, preferred_element_type=F32)


def dot_nt(a, b):
    return lax.dot_general(a, b, (((1,), (1,)), ((), ())), preferred_element_type=F32)


def split(x):
    high = x.astype(BF16)
    return high, (x - high.astype(F32)).astype(BF16)


def mixer(
    dims,
    fq_hbm, fk_hbm, v_hbm, wq_hbm, wk_hbm, wv_hbm, gain, ea_hbm, eb_hbm, eaq_hbm, ebq_hbm, sk_hbm, sq_hbm,
    out,
    fq, fk, v, wq, wk, wv, ea, eb, eaq, ebq, sk, sq,
    edge_k, edge_v, first_state, total, got, chip_sum, gathered, prefixes, arrived, payload, before,
    fq_rows, local, window, map_q, power_own, power_all, squares,
    in_sem, send_sem, recv_sem,
):
    seq_n, head_n, z_n, heads, tokens, normal_row = dims
    x_n = seq_n // 2 // z_n
    chips = seq_n // 2
    half = heads // 2
    pieces = half * PIECES
    blocks = tokens // BLOCK
    me, head = lax.axis_index("seq"), lax.axis_index("head")
    core = lax.rem(me, 2)
    chip = me // 2
    other = me + 1 - 2 * core

    def load(index, src, dst):
        return pltpu.make_async_copy(src, dst, in_sem.at[index])

    first_loads = [load(0, fk_hbm, fk.at[pl.ds(0, heads * FEAT)]), load(1, ea_hbm, ea), load(2, eb_hbm, eb), load(3, sk_hbm, sk)]
    first_loads.append(load(4, v_hbm, v))
    later_loads = [
        load(5, fq_hbm, fq.at[pl.ds(0, heads * FEAT)]), load(6, sq_hbm, sq), load(10, eaq_hbm, eaq), load(11, ebq_hbm, ebq),
        load(7, wk_hbm, wk), load(8, wq_hbm, wq), load(9, wv_hbm, wv),
    ]

    def remote(src, dst, index, seq, group):
        return pltpu.make_async_remote_copy(
            src_ref=src, dst_ref=dst, send_sem=send_sem.at[index], recv_sem=recv_sem.at[index],
            device_id=(seq, group), device_id_type=MESH,
        )

    def settle(buffer, count, sem, rows=PIECE):
        part = buffer.at[pl.ds(0, count), pl.ds(0, rows)]
        pltpu.make_async_copy(part, part, sem).wait()

    barrier = pltpu.get_barrier_semaphore()
    edge_mate = lax.rem(me + 2 * core - 1 + seq_n, seq_n)

    def greet(seq, group):
        pl.semaphore_signal(barrier, inc=1, device_id=(seq, group), device_id_type=MESH)

    for copy in first_loads:
        copy.start()
    x, z = chip // z_n, lax.rem(chip, z_n)
    away = sorted(
        ((dx, dz) for dx in range(x_n) for dz in range(z_n) if dx or dz),
        key=lambda d: -(min(d[0], x_n - d[0]) + 1.01 * min(d[1], z_n - d[1])),
    )
    others = [lax.rem(x + dx, x_n) * z_n + lax.rem(z + dz, z_n) for dx, dz in away]
    for there in others:
        greet(2 * there + core, head)
    greet(other, head)
    greet(edge_mate, head)
    for step in range(1, head_n):
        greet(me, lax.rem(head + step, head_n))

    row_ids = lax.broadcasted_iota(jnp.int32, (ROWS, HD), 0)
    spots = row_ids + row_ids // PIECE * (SLOT - PIECE) - lax.broadcasted_iota(jnp.int32, (ROWS, HD), 1)
    ones_v = jnp.ones((BLOCK, HD), BF16)
    feats = heads * FEAT
    tail = jnp.where(lax.broadcasted_iota(jnp.int32, (128 - feats, tokens), 0) == 0, 1.0, 0.0).astype(BF16)
    fk[pl.ds(feats, 128 - feats), :] = tail
    fq[pl.ds(feats, 128 - feats), :] = tail
    for copy in first_loads:
        copy.wait()
    for copy in later_loads:
        copy.start()

    def put(ref, h, state):
        for piece in range(PIECES):
            ref[h * PIECES + piece, 0:PIECE, :] = state[piece * PIECE : (piece + 1) * PIECE]

    def state_of(h):
        cols = pl.ds(pl.multiple_of(h * HD, HD), HD)
        summed = None
        for block in range(blocks):
            keys = fk[:, pl.ds(block * BLOCK, BLOCK)]
            scale = sk[...]
            mapped = dot(ea[h], keys) * dot(eb[h], keys)
            mapped = (mapped * jnp.concatenate([scale] * (BLOCK // 128), axis=1)).astype(BF16)
            both = dot(mapped, jnp.concatenate([v[pl.ds(block * BLOCK, BLOCK), cols], ones_v], axis=1))
            state, normal = both[:, :HD], both[:, HD:]
            low = jnp.sum(jnp.where(spots == 0, normal, 0.0), axis=0, keepdims=True)
            high = jnp.sum(jnp.where(spots == HD, normal, 0.0), axis=0, keepdims=True)
            state = jnp.where(row_ids == normal_row, low, jnp.where(row_ids == normal_row + 1, high, state))
            if block == 0:
                put(first_state, h, state)
            summed = state if summed is None else summed + state
        put(total, h, summed)

    def states(start):
        def body(i, carry):
            state_of(start + i)
            return carry
        lax.fori_loop(0, half, body, 0, unroll=True)

    states(half * (1 - core))
    pl.semaphore_wait(barrier, 1 + 1 + head_n - 1 + chips - 1)
    swap_out = remote(total.at[pl.ds((1 - core) * pieces, pieces), pl.ds(0, PIECE)], got.at[:, pl.ds(0, PIECE)], 0, other, head)
    swap_out.start()
    states(half * core)

    following = lax.rem(me + 1, seq_n)
    edges = [
        remote(wk_hbm.at[pl.ds(tokens - W, W)], edge_k, 1, following, head),
        remote(wv_hbm.at[pl.ds(tokens - W, W)], edge_v, 2, following, head),
    ]
    swap_out.wait_recv()
    own = pl.ds(core * pieces, pieces)
    chip_sum[...] = total[own] + got[...]

    def to_chips(src, dst, index):
        for there in others:
            remote(src.at[there, pl.ds(0, PIECE)], dst.at[chip, pl.ds(0, PIECE)], index, 2 * there + core, head).start()
        dst[chip] = src[chip]

    to_chips(chip_sum, gathered, 3)
    for copy in edges:
        copy.start()

    for copy in later_loads:
        copy.wait()
    quarter = BLOCK // 2
    tri = lax.broadcasted_iota(jnp.int32, (quarter, quarter), 0) >= lax.broadcasted_iota(jnp.int32, (quarter, quarter), 1)
    feat_lane = lax.broadcasted_iota(jnp.int32, (1, 128), 1)
    fq_rows[...] = fq[...].T

    def within(i, carry):
        h, block = i // blocks, lax.rem(i, blocks)
        cols = pl.ds(pl.multiple_of(h * HD, HD), HD)
        start = pl.multiple_of(block * BLOCK, BLOCK)
        keys = fk[:, pl.ds(start, BLOCK)]
        mine = jnp.where(feat_lane // FEAT == h, 1.0, 0.0).astype(BF16)
        ext = fq_rows[pl.ds(start, BLOCK), :]
        queries = ext * mine
        vals = jnp.concatenate([v[pl.ds(start, BLOCK), cols], ones_v], axis=1)

        def weights(q, k):
            s = dot(q, k)
            return 1.0 + s * 0.25 + s * s * (1.0 / 32.0)

        top = jnp.where(tri, weights(queries[:quarter], keys[:, :quarter]), 0.0).astype(BF16)
        local[h, pl.ds(start, quarter), :] = dot(top, vals[:quarter])
        left = weights(queries[quarter:], keys[:, :quarter]).astype(BF16)
        right = jnp.where(tri, weights(queries[quarter:], keys[:, quarter:]), 0.0).astype(BF16)
        local[h, pl.ds(start + quarter, quarter), :] = dot(jnp.concatenate([left, right], axis=1), vals)
        mapped = dot_nt(ext, eaq[h]) * dot_nt(ext, ebq[h]) * sq[0:1, :]
        map_q[h, pl.ds(start, BLOCK), :] = mapped.astype(BF16)
        return carry

    lax.fori_loop(0, heads * blocks, within, 0, unroll=4)

    spot = normal_row // PIECE * SLOT + normal_row % PIECE

    used = lax.broadcasted_iota(jnp.int32, (PIECES, SLOT, HD), 1) < PIECE

    def state_halves(ref, h):
        state = jnp.where(used, ref[pl.ds(h * PIECES, PIECES)], 0.0).reshape(WIDE, HD)
        normal = jnp.concatenate(
            [jnp.broadcast_to(state[spot + i : spot + i + 1], (HD, HD)) for i in range(2)], axis=1
        )
        return jnp.concatenate(split(state), axis=1), jnp.concatenate(split(normal), axis=0)

    def apply_state(mapped, halves):
        upper, lower = dot(mapped, halves[0]), dot_nt(mapped, halves[1])
        return jnp.concatenate([upper[:, :HD] + upper[:, HD:], lower[:, :HD] + lower[:, HD:]], axis=1)

    def first_block(h, carry):
        rows = pl.ds(BLOCK, BLOCK)
        local[h, rows, :] += apply_state(map_q[h, rows, :], state_halves(first_state, h))
        return carry

    lax.fori_loop(0, heads, first_block, 0, unroll=2)

    band_row = lax.broadcasted_iota(jnp.int32, (W, 2 * W), 0)
    band_col = lax.broadcasted_iota(jnp.int32, (W, 2 * W), 1)
    band = (band_col > band_row) & (band_col <= band_row + W)
    sharp = 1.0 / math.sqrt(HD)

    def attend(scores, allowed):
        scores = jnp.where(allowed, scores * sharp, -1e30)
        weights = jnp.exp(scores - jnp.max(scores, axis=1, keepdims=True))
        return (weights / jnp.sum(weights, axis=1, keepdims=True)).astype(BF16)

    group = 8
    band_group = jnp.concatenate([band] * group, axis=0)

    def windows(h, first, count):
        cols = pl.ds(pl.multiple_of(h * HD, HD), HD)
        starts = [first + c * W for c in range(count)]
        scores = [
            dot_nt(wq[pl.ds(s, W), cols], wk[pl.ds(s - W, 2 * W), cols]) for s in starts
        ]
        probs = attend(jnp.concatenate(scores, axis=0), band_group[: count * W])
        for c, s in enumerate(starts):
            window[pl.ds(s, W), cols] = dot(probs[c * W : (c + 1) * W], wv[pl.ds(s - W, 2 * W), cols])

    def window_head(h, carry):
        windows(h, W, group - 1)

        def rest(g, inner):
            windows(h, pl.multiple_of(g * group * W, group * W), group)
            return inner

        return lax.fori_loop(1, tokens // (group * W), rest, carry, unroll=True)

    settle(gathered, chips - 1, recv_sem.at[3])

    def add(u, run):
        prefixes[u] = run
        return run + gathered[u]

    lax.fori_loop(0, chips, add, jnp.zeros((SLOT, HD), F32), unroll=8)
    to_chips(prefixes, arrived, 4)

    lax.fori_loop(0, heads, window_head, 0)

    edges[0].wait_recv()
    edges[1].wait_recv()
    band_first = band & ((band_col >= W) | (me > 0))

    def window_edge(h, carry):
        cols = pl.ds(pl.multiple_of(h * HD, HD), HD)
        keys = jnp.concatenate([edge_k[:, cols], wk[pl.ds(0, W), cols]], axis=0)
        vals = jnp.concatenate([edge_v[:, cols], wv[pl.ds(0, W), cols]], axis=0)
        probs = attend(dot_nt(wq[pl.ds(0, W), cols], keys), band_first)
        window[pl.ds(0, W), cols] = dot(probs, vals)
        return carry

    lax.fori_loop(0, heads, window_edge, 0, unroll=True)

    ahead = jnp.where(core == 0, 1.0, 0.0)

    @pl.when(chip > 0)
    def _():
        settle(arrived, chips - 1, recv_sem.at[4])
        payload[...] = arrived[...] + total[own] * ahead
        before[own] = arrived[...] + got[...] * (1.0 - ahead)

    @pl.when(chip == 0)
    def _():
        payload[...] = total[own] * ahead
        before[own] = got[...] * (1.0 - ahead)

    swap_back = remote(payload.at[:, pl.ds(0, PIECE)], before.at[pl.ds(core * pieces, pieces), pl.ds(0, PIECE)], 5, other, head)
    swap_back.start()

    def finish(h, block, halves, fresh):
        cols = pl.ds(pl.multiple_of(h * HD, HD), HD)
        rows = pl.ds(block * BLOCK, BLOCK)
        sums = apply_state(map_q[h, rows, :], halves) + local[h, rows, :]
        combined = gain[h] * (sums[:, :HD] / sums[:, HD:] + window[rows, cols])
        window[rows, cols] = combined
        squared = combined * combined
        squares[rows, :] = squared if fresh else squares[rows, :] + squared

    for i in range(half):
        h = half * core + i
        halves = state_halves(before, h)
        for block in range(blocks):
            finish(h, block, halves, i == 0)
    swap_back.wait_recv()
    rest = [half * (1 - core) + i for i in range(half)]
    rest_halves = [state_halves(before, h) for h in rest]
    for block in range(blocks):
        for h, halves in zip(rest, rest_halves):
            finish(h, block, halves, False)
        for r in range(BLOCK // 128):
            turned = squares[pl.ds(block * BLOCK + r * 128, 128), :].T
            power_own[block, r : r + 1, :] = jnp.sum(turned, axis=0, keepdims=True)
        power_all[block, head] = power_own[block]
        for step in range(1, head_n):
            remote(
                power_own.at[block], power_all.at[block, head], 6 + block, me, lax.rem(head + step, head_n)
            ).start()

    for block in range(blocks):
        settle(power_all.at[block], head_n - 1, recv_sem.at[6 + block], BLOCK // 128)
        power = jnp.sum(power_all[block], axis=0) * (1.0 / (heads * head_n * HD))
        factor = lax.rsqrt(power + EPS)
        for r in range(BLOCK // 128):
            some = pl.ds(block * BLOCK + r * 128, 128)
            column = jnp.broadcast_to(factor[r : r + 1], (128, 128)).T
            out[some, :] = (window[some, :] * jnp.concatenate([column] * heads, axis=1)).astype(BF16)

    @pl.when(chip == 0)
    def _():
        settle(arrived, chips - 1, recv_sem.at[4])

    swap_out.wait_send()
    for copy in edges:
        copy.wait_send()
    swap_back.wait_send()

    settle(gathered, chips - 1, send_sem.at[3])
    settle(arrived, chips - 1, send_sem.at[4])
    for block in range(blocks):
        settle(power_all.at[block], head_n - 1, send_sem.at[6 + block], BLOCK // 128)


def solution(mesh):
    seq_n, head_n = mesh.shape["seq"], mesh.shape["head"]
    z_n = 8

    def local(feat_q, feat_k, values, win_q, win_k, win_v, head_gain):
        tokens, width = values.shape
        heads = head_gain.shape[0]
        *tables, normal_row = feature_tables(heads)
        chips = seq_n // 2
        pieces = heads // 2 * PIECES
        blocks = tokens // BLOCK
        dims = (seq_n, head_n, z_n, heads, tokens, normal_row)
        anywhere = pl.BlockSpec(memory_space=pltpu.HBM)
        vm = pltpu.VMEM
        stay = functools.partial(pltpu.with_memory_space_constraint, memory_space=pltpu.HBM)
        return pl.pallas_call(
            functools.partial(mixer, dims),
            out_shape=jax.ShapeDtypeStruct((tokens, width), BF16),
            in_specs=[anywhere] * 6 + [pl.BlockSpec(memory_space=pltpu.SMEM)] + [anywhere] * 6,
            out_specs=pl.BlockSpec(memory_space=pltpu.VMEM),
            scratch_shapes=[
                vm((128, tokens), BF16), vm((128, tokens), BF16),
                vm(values.shape, BF16), vm(values.shape, BF16), vm(values.shape, BF16), vm(values.shape, BF16),
                vm((heads, ROWS, 128), BF16), vm((heads, ROWS, 128), BF16),
                vm((heads, WIDE, 128), BF16), vm((heads, WIDE, 128), BF16), vm((ROWS, 128), F32), vm((8, WIDE), F32),
                vm((W, width), BF16), vm((W, width), BF16),
                vm((2 * pieces, SLOT, HD), F32),
                vm((2 * pieces, SLOT, HD), F32),
                vm((pieces, SLOT, HD), F32),
                vm((pieces, SLOT, HD), F32),
                vm((chips, SLOT, HD), F32),
                vm((chips, SLOT, HD), F32),
                vm((pieces, SLOT, HD), F32),
                vm((pieces, SLOT, HD), F32),
                vm((2 * pieces, SLOT, HD), F32),
                vm((tokens, 128), BF16),
                vm((heads, tokens, 2 * HD), F32),
                vm((tokens, width), F32),
                vm((heads, tokens, WIDE), BF16),
                vm((blocks, BLOCK // 128, 128), F32),
                vm((blocks, head_n, BLOCK // 128, 128), F32),
                vm((tokens, HD), F32),
                pltpu.SemaphoreType.DMA((12,)),
                pltpu.SemaphoreType.DMA((6 + blocks,)),
                pltpu.SemaphoreType.DMA((6 + blocks,)),
            ],
            compiler_params=pltpu.CompilerParams(
                collective_id=0, has_side_effects=True, vmem_limit_bytes=48 * 2**20
            ),
            name="mixer",
        )(
            *(stay(x) for x in (feat_q.T, feat_k.T, values, win_q, win_k, win_v, head_gain)),
            *(stay(x) for x in (
                *(jnp.asarray(table, BF16) for table in tables[:4]), *(jnp.asarray(table) for table in tables[4:]),
            )),
        )

    placed = (P("seq", "head"),) * 6 + (P("head"),)
    return jax.shard_map(local, mesh=mesh, in_specs=placed, out_specs=P("seq", "head"), check_vma=False)
```

```python
import functools
import math

import jax
import jax.numpy as jnp
import numpy as np
from jax import lax
from jax.experimental import pallas as pl
from jax.experimental.pallas import tpu as pltpu
from jax.sharding import PartitionSpec as P

MESH = pl.DeviceIdType.MESH
F32 = jnp.float32
BF16 = jnp.bfloat16

W = 64
BLOCK = 512
FEAT = 16
HD = 128
ROWS = 160
PIECE = 10
SLOT = 16
PIECES = ROWS // PIECE
WIDE = PIECES * SLOT
QUAD = 1.0 / (4.0 * math.sqrt(2.0))
EPS = 1e-06


def feature_tables(heads):
    ones_lane = heads * FEAT
    first = np.zeros((heads, ROWS, 128), np.float32)
    second = np.zeros((heads, ROWS, 128), np.float32)
    scale_k = np.zeros((ROWS,), np.float32)
    scale_q = np.zeros((ROWS,), np.float32)
    row = 0
    for shift in range(FEAT // 2 + 1):
        for a in range(FEAT if shift < FEAT // 2 else FEAT // 2):
            for h in range(heads):
                first[h, row, h * FEAT + a] = 1.0
                second[h, row, h * FEAT + (a + shift) % FEAT] = 1.0
            scale_k[row] = QUAD
            scale_q[row] = np.float32(QUAD) * (1.0 if shift == 0 else 2.0)
            row += 1
    for a in range(FEAT):
        for h in range(heads):
            first[h, row, h * FEAT + a] = 1.0
            second[h, row, ones_lane] = 1.0
        scale_k[row] = scale_q[row] = 0.5
        row += 1
    first[:, row, ones_lane] = 1.0
    second[:, row, ones_lane] = 1.0
    scale_k[row] = scale_q[row] = 1.0
    row += 1
    assert row + 2 <= ROWS
    spot = np.arange(ROWS) // PIECE * SLOT + np.arange(ROWS) % PIECE
    first_q = np.zeros((heads, WIDE, 128), np.float32)
    second_q = np.zeros((heads, WIDE, 128), np.float32)
    first_q[:, spot], second_q[:, spot] = first, second
    wide_k = np.ascontiguousarray(np.broadcast_to(scale_k[:, None], (ROWS, 128)))
    wide_q = np.zeros((8, WIDE), np.float32)
    wide_q[:, spot] = scale_q
    return first, second, first_q, second_q, wide_k, wide_q, row


def dot(a, b):
    return jnp.dot(a, b, preferred_element_type=F32)


def dot_nt(a, b):
    return lax.dot_general(a, b, (((1,), (1,)), ((), ())), preferred_element_type=F32)


def split(x):
    high = x.astype(BF16)
    return high, (x - high.astype(F32)).astype(BF16)


def mixer(
    dims,
    fq_hbm, fk_hbm, v_hbm, wq_hbm, wk_hbm, wv_hbm, gain, ea_hbm, eb_hbm, eaq_hbm, ebq_hbm, sk_hbm, sq_hbm,
    out,
    fq, fk, v, wq, wk, wv, ea, eb, eaq, ebq, sk, sq,
    edge_k, edge_v, first_state, total, got, chip_sum, gathered, prefixes, arrived, payload, before,
    fq_rows, local, window, map_q, power_own, power_all, squares,
    in_sem, send_sem, recv_sem,
):
    seq_n, head_n, z_n, heads, tokens, normal_row = dims
    x_n = seq_n // 2 // z_n
    chips = seq_n // 2
    half = heads // 2
    pieces = half * PIECES
    blocks = tokens // BLOCK
    me, head = lax.axis_index("seq"), lax.axis_index("head")
    core = lax.rem(me, 2)
    chip = me // 2
    other = me + 1 - 2 * core

    def load(index, src, dst):
        return pltpu.make_async_copy(src, dst, in_sem.at[index])

    first_loads = [load(0, fk_hbm, fk.at[pl.ds(0, heads * FEAT)]), load(1, ea_hbm, ea), load(2, eb_hbm, eb), load(3, sk_hbm, sk)]
    first_loads.append(load(4, v_hbm, v))
    later_loads = [
        load(5, fq_hbm, fq.at[pl.ds(0, heads * FEAT)]), load(6, sq_hbm, sq), load(10, eaq_hbm, eaq), load(11, ebq_hbm, ebq),
        load(7, wk_hbm, wk), load(8, wq_hbm, wq), load(9, wv_hbm, wv),
    ]

    def remote(src, dst, index, seq, group):
        return pltpu.make_async_remote_copy(
            src_ref=src, dst_ref=dst, send_sem=send_sem.at[index], recv_sem=recv_sem.at[index],
            device_id=(seq, group), device_id_type=MESH,
        )

    def settle(buffer, count, sem, rows=PIECE):
        part = buffer.at[pl.ds(0, count), pl.ds(0, rows)]
        pltpu.make_async_copy(part, part, sem).wait()

    barrier = pltpu.get_barrier_semaphore()
    edge_mate = lax.rem(me + 2 * core - 1 + seq_n, seq_n)

    def greet(seq, group):
        pl.semaphore_signal(barrier, inc=1, device_id=(seq, group), device_id_type=MESH)

    for copy in first_loads:
        copy.start()
    x, z = chip // z_n, lax.rem(chip, z_n)
    away = sorted(
        ((dx, dz) for dx in range(x_n) for dz in range(z_n) if dx or dz),
        key=lambda d: -(min(d[0], x_n - d[0]) + 1.01 * min(d[1], z_n - d[1])),
    )
    others = [lax.rem(x + dx, x_n) * z_n + lax.rem(z + dz, z_n) for dx, dz in away]
    for there in others:
        greet(2 * there + core, head)
    greet(other, head)
    greet(edge_mate, head)
    for step in range(1, head_n):
        greet(me, lax.rem(head + step, head_n))

    row_ids = lax.broadcasted_iota(jnp.int32, (ROWS, HD), 0)
    spots = row_ids + row_ids // PIECE * (SLOT - PIECE) - lax.broadcasted_iota(jnp.int32, (ROWS, HD), 1)
    ones_v = jnp.ones((BLOCK, HD), BF16)
    feats = heads * FEAT
    tail = jnp.where(lax.broadcasted_iota(jnp.int32, (128 - feats, tokens), 0) == 0, 1.0, 0.0).astype(BF16)
    fk[pl.ds(feats, 128 - feats), :] = tail
    fq[pl.ds(feats, 128 - feats), :] = tail
    for copy in first_loads:
        copy.wait()
    for copy in later_loads:
        copy.start()

    def put(ref, h, state):
        for piece in range(PIECES):
            ref[h * PIECES + piece, 0:PIECE, :] = state[piece * PIECE : (piece + 1) * PIECE]

    def state_of(h):
        cols = pl.ds(pl.multiple_of(h * HD, HD), HD)
        summed = None
        for block in range(blocks):
            keys = fk[:, pl.ds(block * BLOCK, BLOCK)]
            scale = sk[...]
            mapped = dot(ea[h], keys) * dot(eb[h], keys)
            mapped = (mapped * jnp.concatenate([scale] * (BLOCK // 128), axis=1)).astype(BF16)
            both = dot(mapped, jnp.concatenate([v[pl.ds(block * BLOCK, BLOCK), cols], ones_v], axis=1))
            state, normal = both[:, :HD], both[:, HD:]
            low = jnp.sum(jnp.where(spots == 0, normal, 0.0), axis=0, keepdims=True)
            high = jnp.sum(jnp.where(spots == HD, normal, 0.0), axis=0, keepdims=True)
            state = jnp.where(row_ids == normal_row, low, jnp.where(row_ids == normal_row + 1, high, state))
            if block == 0:
                put(first_state, h, state)
            summed = state if summed is None else summed + state
        put(total, h, summed)

    def states(start):
        def body(i, carry):
            state_of(start + i)
            return carry
        lax.fori_loop(0, half, body, 0, unroll=True)

    states(half * (1 - core))
    pl.semaphore_wait(barrier, 1 + 1 + head_n - 1 + chips - 1)
    swap_out = remote(total.at[pl.ds((1 - core) * pieces, pieces), pl.ds(0, PIECE)], got.at[:, pl.ds(0, PIECE)], 0, other, head)
    swap_out.start()
    states(half * core)

    following = lax.rem(me + 1, seq_n)
    edges = [
        remote(wk_hbm.at[pl.ds(tokens - W, W)], edge_k, 1, following, head),
        remote(wv_hbm.at[pl.ds(tokens - W, W)], edge_v, 2, following, head),
    ]
    swap_out.wait_recv()
    own = pl.ds(core * pieces, pieces)
    chip_sum[...] = total[own] + got[...]

    by_z = sorted(away, key=lambda d: (-min(d[1], z_n - d[1]), -min(d[0], x_n - d[0])))
    by_z = [lax.rem(x + dx, x_n) * z_n + lax.rem(z + dz, z_n) for dx, dz in by_z]

    def to_chips(src, dst, index):
        for there in by_z:
            remote(src.at[there, pl.ds(0, PIECE)], dst.at[chip, pl.ds(0, PIECE)], index, 2 * there + core, head).start()
        dst[chip] = src[chip]

    to_chips(chip_sum, gathered, 3)
    for copy in edges:
        copy.start()

    for copy in later_loads:
        copy.wait()
    quarter = BLOCK // 2
    tri = lax.broadcasted_iota(jnp.int32, (quarter, quarter), 0) >= lax.broadcasted_iota(jnp.int32, (quarter, quarter), 1)
    feat_lane = lax.broadcasted_iota(jnp.int32, (1, 128), 1)
    fq_rows[...] = fq[...].T

    def within(i, carry):
        h, block = i // blocks, lax.rem(i, blocks)
        cols = pl.ds(pl.multiple_of(h * HD, HD), HD)
        start = pl.multiple_of(block * BLOCK, BLOCK)
        keys = fk[:, pl.ds(start, BLOCK)]
        mine = jnp.where(feat_lane // FEAT == h, 1.0, 0.0).astype(BF16)
        ext = fq_rows[pl.ds(start, BLOCK), :]
        queries = ext * mine
        vals = jnp.concatenate([v[pl.ds(start, BLOCK), cols], ones_v], axis=1)

        def weights(q, k):
            s = dot(q, k)
            return 1.0 + s * 0.25 + s * s * (1.0 / 32.0)

        top = jnp.where(tri, weights(queries[:quarter], keys[:, :quarter]), 0.0).astype(BF16)
        local[h, pl.ds(start, quarter), :] = dot(top, vals[:quarter])
        left = weights(queries[quarter:], keys[:, :quarter]).astype(BF16)
        right = jnp.where(tri, weights(queries[quarter:], keys[:, quarter:]), 0.0).astype(BF16)
        local[h, pl.ds(start + quarter, quarter), :] = dot(jnp.concatenate([left, right], axis=1), vals)
        mapped = dot_nt(ext, eaq[h]) * dot_nt(ext, ebq[h]) * sq[0:1, :]
        map_q[h, pl.ds(start, BLOCK), :] = mapped.astype(BF16)
        return carry

    lax.fori_loop(0, heads * blocks, within, 0, unroll=4)

    spot = normal_row // PIECE * SLOT + normal_row % PIECE

    used = lax.broadcasted_iota(jnp.int32, (PIECES, SLOT, HD), 1) < PIECE

    def state_halves(ref, h):
        state = jnp.where(used, ref[pl.ds(h * PIECES, PIECES)], 0.0).reshape(WIDE, HD)
        normal = jnp.concatenate(
            [jnp.broadcast_to(state[spot + i : spot + i + 1], (HD, HD)) for i in range(2)], axis=1
        )
        return jnp.concatenate(split(state), axis=1), jnp.concatenate(split(normal), axis=0)

    def apply_state(mapped, halves):
        upper, lower = dot(mapped, halves[0]), dot_nt(mapped, halves[1])
        return jnp.concatenate([upper[:, :HD] + upper[:, HD:], lower[:, :HD] + lower[:, HD:]], axis=1)

    def first_block(h, carry):
        rows = pl.ds(BLOCK, BLOCK)
        local[h, rows, :] += apply_state(map_q[h, rows, :], state_halves(first_state, h))
        return carry

    lax.fori_loop(0, heads, first_block, 0, unroll=2)

    band_row = lax.broadcasted_iota(jnp.int32, (W, 2 * W), 0)
    band_col = lax.broadcasted_iota(jnp.int32, (W, 2 * W), 1)
    band = (band_col > band_row) & (band_col <= band_row + W)
    sharp = 1.0 / math.sqrt(HD)

    def attend(scores, allowed):
        scores = jnp.where(allowed, scores * sharp, -1e30)
        weights = jnp.exp(scores - jnp.max(scores, axis=1, keepdims=True))
        return (weights / jnp.sum(weights, axis=1, keepdims=True)).astype(BF16)

    group = 8
    band_group = jnp.concatenate([band] * group, axis=0)

    def windows(h, first, count):
        cols = pl.ds(pl.multiple_of(h * HD, HD), HD)
        starts = [first + c * W for c in range(count)]
        scores = [
            dot_nt(wq[pl.ds(s, W), cols], wk[pl.ds(s - W, 2 * W), cols]) for s in starts
        ]
        probs = attend(jnp.concatenate(scores, axis=0), band_group[: count * W])
        for c, s in enumerate(starts):
            window[pl.ds(s, W), cols] = dot(probs[c * W : (c + 1) * W], wv[pl.ds(s - W, 2 * W), cols])

    def window_head(h, carry):
        windows(h, W, group - 1)

        def rest(g, inner):
            windows(h, pl.multiple_of(g * group * W, group * W), group)
            return inner

        return lax.fori_loop(1, tokens // (group * W), rest, carry, unroll=True)

    settle(gathered, chips - 1, recv_sem.at[3])

    def add(u, run):
        prefixes[u] = run
        return run + gathered[u]

    lax.fori_loop(0, chips, add, jnp.zeros((SLOT, HD), F32), unroll=8)
    to_chips(prefixes, arrived, 4)

    lax.fori_loop(0, heads, window_head, 0)

    edges[0].wait_recv()
    edges[1].wait_recv()
    band_first = band & ((band_col >= W) | (me > 0))

    def window_edge(h, carry):
        cols = pl.ds(pl.multiple_of(h * HD, HD), HD)
        keys = jnp.concatenate([edge_k[:, cols], wk[pl.ds(0, W), cols]], axis=0)
        vals = jnp.concatenate([edge_v[:, cols], wv[pl.ds(0, W), cols]], axis=0)
        probs = attend(dot_nt(wq[pl.ds(0, W), cols], keys), band_first)
        window[pl.ds(0, W), cols] = dot(probs, vals)
        return carry

    lax.fori_loop(0, heads, window_edge, 0, unroll=True)

    ahead = jnp.where(core == 0, 1.0, 0.0)

    @pl.when(chip > 0)
    def _():
        settle(arrived, chips - 1, recv_sem.at[4])
        payload[...] = arrived[...] + total[own] * ahead
        before[own] = arrived[...] + got[...] * (1.0 - ahead)

    @pl.when(chip == 0)
    def _():
        payload[...] = total[own] * ahead
        before[own] = got[...] * (1.0 - ahead)

    swap_back = remote(payload.at[:, pl.ds(0, PIECE)], before.at[pl.ds(core * pieces, pieces), pl.ds(0, PIECE)], 5, other, head)
    swap_back.start()

    def finish(h, block, halves, fresh):
        cols = pl.ds(pl.multiple_of(h * HD, HD), HD)
        rows = pl.ds(block * BLOCK, BLOCK)
        sums = apply_state(map_q[h, rows, :], halves) + local[h, rows, :]
        combined = gain[h] * (sums[:, :HD] / sums[:, HD:] + window[rows, cols])
        window[rows, cols] = combined
        squared = combined * combined
        squares[rows, :] = squared if fresh else squares[rows, :] + squared

    for i in range(half):
        h = half * core + i
        halves = state_halves(before, h)
        for block in range(blocks):
            finish(h, block, halves, i == 0)
    swap_back.wait_recv()
    rest = [half * (1 - core) + i for i in range(half)]
    rest_halves = [state_halves(before, h) for h in rest]
    for block in range(blocks):
        for h, halves in zip(rest, rest_halves):
            finish(h, block, halves, False)
        for r in range(BLOCK // 128):
            turned = squares[pl.ds(block * BLOCK + r * 128, 128), :].T
            q = block * BLOCK // 128 + r
            power_own[q : q + 1, :] = jnp.sum(turned, axis=0, keepdims=True)
    power_all[head] = power_own[...]
    for step in range(1, head_n):
        remote(power_own, power_all.at[head], 6, me, lax.rem(head + step, head_n)).start()

    settle(power_all, head_n - 1, recv_sem.at[6], tokens // 128)
    factor = lax.rsqrt(jnp.sum(power_all[...], axis=0) * (1.0 / (heads * head_n * HD)) + EPS)
    for r in range(tokens // 128):
        some = pl.ds(r * 128, 128)
        column = jnp.broadcast_to(factor[r : r + 1], (128, 128)).T
        out[some, :] = (window[some, :] * jnp.concatenate([column] * heads, axis=1)).astype(BF16)

    @pl.when(chip == 0)
    def _():
        settle(arrived, chips - 1, recv_sem.at[4])

    swap_out.wait_send()
    for copy in edges:
        copy.wait_send()
    swap_back.wait_send()

    settle(gathered, chips - 1, send_sem.at[3])
    settle(arrived, chips - 1, send_sem.at[4])
    settle(power_all, head_n - 1, send_sem.at[6], tokens // 128)


def solution(mesh):
    seq_n, head_n = mesh.shape["seq"], mesh.shape["head"]
    z_n = 8

    def local(feat_q, feat_k, values, win_q, win_k, win_v, head_gain):
        tokens, width = values.shape
        heads = head_gain.shape[0]
        *tables, normal_row = feature_tables(heads)
        chips = seq_n // 2
        pieces = heads // 2 * PIECES
        blocks = tokens // BLOCK
        dims = (seq_n, head_n, z_n, heads, tokens, normal_row)
        anywhere = pl.BlockSpec(memory_space=pltpu.HBM)
        vm = pltpu.VMEM
        stay = functools.partial(pltpu.with_memory_space_constraint, memory_space=pltpu.HBM)
        return pl.pallas_call(
            functools.partial(mixer, dims),
            out_shape=jax.ShapeDtypeStruct((tokens, width), BF16),
            in_specs=[anywhere] * 6 + [pl.BlockSpec(memory_space=pltpu.SMEM)] + [anywhere] * 6,
            out_specs=pl.BlockSpec(memory_space=pltpu.VMEM),
            scratch_shapes=[
                vm((128, tokens), BF16), vm((128, tokens), BF16),
                vm(values.shape, BF16), vm(values.shape, BF16), vm(values.shape, BF16), vm(values.shape, BF16),
                vm((heads, ROWS, 128), BF16), vm((heads, ROWS, 128), BF16),
                vm((heads, WIDE, 128), BF16), vm((heads, WIDE, 128), BF16), vm((ROWS, 128), F32), vm((8, WIDE), F32),
                vm((W, width), BF16), vm((W, width), BF16),
                vm((2 * pieces, SLOT, HD), F32),
                vm((2 * pieces, SLOT, HD), F32),
                vm((pieces, SLOT, HD), F32),
                vm((pieces, SLOT, HD), F32),
                vm((chips, SLOT, HD), F32),
                vm((chips, SLOT, HD), F32),
                vm((pieces, SLOT, HD), F32),
                vm((pieces, SLOT, HD), F32),
                vm((2 * pieces, SLOT, HD), F32),
                vm((tokens, 128), BF16),
                vm((heads, tokens, 2 * HD), F32),
                vm((tokens, width), F32),
                vm((heads, tokens, WIDE), BF16),
                vm((tokens // 128, 128), F32),
                vm((head_n, tokens // 128, 128), F32),
                vm((tokens, HD), F32),
                pltpu.SemaphoreType.DMA((12,)),
                pltpu.SemaphoreType.DMA((6 + blocks,)),
                pltpu.SemaphoreType.DMA((6 + blocks,)),
            ],
            compiler_params=pltpu.CompilerParams(
                collective_id=0, has_side_effects=True, vmem_limit_bytes=48 * 2**20
            ),
            name="mixer",
        )(
            *(stay(x) for x in (feat_q.T, feat_k.T, values, win_q, win_k, win_v, head_gain)),
            *(stay(x) for x in (
                *(jnp.asarray(table, BF16) for table in tables[:4]), *(jnp.asarray(table) for table in tables[4:]),
            )),
        )

    placed = (P("seq", "head"),) * 6 + (P("head"),)
    return jax.shard_map(local, mesh=mesh, in_specs=placed, out_specs=P("seq", "head"), check_vma=False)
```
